256 devices in a mesh: scan: 8 (over y_hi, x), tile: 32 (over y_lo, z, core).
Axes of the slice: x: 4, y: 4 (y_hi: 2, y_lo: 2; y = y_hi * 2 + y_lo), z: 8, core: 2. Of those that a mesh axis runs over, the one named last changes fastest.
Arguments:
- object_slices: bfloat16 [2, 8, 2048, 1024], P(None, None, 'tile'), may hold values from -4 to 4
- probe_wave: bfloat16 [2, 64, 1024], replicated, may hold values from -6 to 6
- propagator: bfloat16 [2, 8, 128, 128], replicated, may hold values from -0.15625 to 0.15625
- offsets: int32 [32, 8], P('tile', 'scan'), may hold values from 0 to 48, as said below
- adjoint: bfloat16 [2, 32, 8, 64, 1024], P(None, 'tile', 'scan'), may hold values from -6 to 6
Outputs:
- updated: float32 [2, 8, 2048, 1024], P(None, 'scan', 'tile')
The draws below stay inside these ranges and needn't reach their ends.
Inputs may be any that keep to these rules, and one draw needn't show every extreme that they name: `offsets`: every offset is a multiple of 16; in the last tile every offset is 0, so no window leaves the object.
All inputs are finite; a program needn't handle non-finite values.
Results may differ from the reference program's by a relative error of at most 0.029.
Values may be sent and summed in bfloat16 or wider, within the bound.
No kernel may reach another device: no remote copies, remote signals or barrier semaphores. Data moves between devices by JAX's collectives and lax.ppermute only.
A program may use at most 64 MiB of HBM per device.

```python
import jax
import jax.numpy as jnp
from jax import lax

ROWS = 64
POS_DEV = 1
BLK = 128
BAND = 8
PR = 64
STRIDE = 16
TV_ITERS = 6
NC = 1024
SLICES = 8
TILES = 32
NR = 2048
POSITIONS = 8
N_SCAN = 8


def draw_offsets(key, part):
    key = jax.random.fold_in(key, 11)
    first_key, second_key = jax.random.split(key)
    steps_all = ROWS // STRIDE
    steps_last = (ROWS - PR) // STRIDE + 1
    general = jax.random.randint(first_key, (TILES, POSITIONS), 0, steps_all, dtype=jnp.int32)
    last_tile = jax.random.randint(second_key, (TILES, POSITIONS), 0, steps_last, dtype=jnp.int32)
    tile_rows = jnp.arange(TILES, dtype=jnp.int32)[:, None]
    chosen = jnp.where(tile_rows == TILES - 1, last_tile, general)
    chosen = chosen.at[0, 0].set(steps_all - 1)
    chosen = chosen.at[TILES - 1, 0].set(steps_last - 1)
    return chosen * STRIDE


def block_scale(key, extent, shards, low, high):
    gain = 1.0
    for axis_at, shards_of in shards:
        steps = jax.random.uniform(jax.random.fold_in(jax.random.fold_in(key, 6), axis_at), (shards_of,), jnp.float32, low / len(shards), high / len(shards))
        gain = gain * jnp.repeat(jnp.exp(steps), extent[axis_at] // shards_of).reshape((-1,) + (1,) * (len(extent) - 1 - axis_at))
    return gain


def centred(stream_key, shape, scale, bound, cuts=(), held_as=jnp.bfloat16):
    values = scale * jax.random.normal(stream_key, shape, jnp.float32)
    if cuts:
        values = values * block_scale(stream_key, shape, cuts, -0.22, 0.18)
    return jnp.clip(values, -bound, bound).astype(held_as)


def setup_inputs(seed: int = 0) -> dict:
    seeds = jax.random.split(jax.random.key(seed), 6)
    return {
        "object_slices": centred(seeds[0], (2, SLICES, NR, NC), 0.7, 4.0, ((2, 32),)),
        "probe_wave": centred(seeds[1], (2, PR, NC), 1.0, 6.0),
        "propagator": centred(seeds[2], (2, BAND, BLK, BLK), (3 * BAND * BLK // 2) ** -0.5, 0.15625),
        "offsets": draw_offsets(jax.random.fold_in(seeds[5], 71), 0),
        "adjoint": centred(seeds[4], (2, TILES, POSITIONS, PR, NC), 1.0, 6.0, ((1, 32), (2, 8))),
    }


STEP_SIZE = 0.5
TV_WEIGHT = 1.0
DUAL_STEP = 0.125
HIGHEST = lax.Precision.HIGHEST

def to_bfloat(values):
    return lax.optimization_barrier(values.astype(jnp.bfloat16)).astype(jnp.float32)

def complex_mul(factor_one, factor_two):
    return jnp.stack([factor_one[0] * factor_two[0] - factor_one[1] * factor_two[1], factor_one[0] * factor_two[1] + factor_one[1] * factor_two[0]])

def mul_conj(factor_one, factor_two):
    return jnp.stack([factor_one[0] * factor_two[0] + factor_one[1] * factor_two[1], factor_one[1] * factor_two[0] - factor_one[0] * factor_two[1]])

def dense_matrix(propagator):
    blocks = NC // BLK
    centre = BAND // 2
    weights = propagator.astype(jnp.float32)
    matrix = jnp.zeros((2, NC, NC), jnp.float32)
    for column_block in range(blocks):
        for offset_block in range(BAND):
            source = column_block + offset_block - centre
            if 0 <= source < blocks:
                matrix = matrix.at[:, source * BLK:(source + 1) * BLK, column_block * BLK:(column_block + 1) * BLK].set(weights[:, offset_block])
    return matrix

def matmul(left_side, right_side):
    return jnp.dot(left_side, right_side, precision=HIGHEST, preferred_element_type=jnp.float32)

def apply_matrix(field, matrix):
    real_part = matmul(field[0], matrix[0]) - matmul(field[1], matrix[1])
    imag_part = matmul(field[0], matrix[1]) + matmul(field[1], matrix[0])
    return jnp.stack([real_part, imag_part])

def apply_adjoint(field, matrix):
    real_part = matmul(field[0], matrix[0].T) + matmul(field[1], matrix[1].T)
    imag_part = matmul(field[1], matrix[0].T) - matmul(field[0], matrix[1].T)
    return jnp.stack([real_part, imag_part])

def window_gradient(patch, probe32, exit_adjoint, matrix):
    waves = []
    wave = probe32
    for layer in range(SLICES):
        waves.append(wave)
        if layer + 1 < SLICES:
            transmitted = to_bfloat(complex_mul(patch[:, layer], wave))
            wave = to_bfloat(apply_matrix(transmitted, matrix))
    upstream = exit_adjoint
    gradients = [None] * SLICES
    for layer in reversed(range(SLICES)):
        before = apply_adjoint(upstream, matrix)
        gradients[layer] = mul_conj(before, waves[layer])
        if layer > 0:
            upstream = to_bfloat(mul_conj(before, patch[:, layer]))
    return jnp.stack(gradients, axis=1)

def divergence(dual_rows, dual_cols, row_above):
    previous = jnp.concatenate([row_above, dual_rows[:, :, :-1]], axis=2)
    shifted = jnp.pad(dual_cols[..., :-1], ((0, 0), (0, 0), (0, 0), (1, 0)))
    return dual_rows - previous + (dual_cols - shifted)

def dual_update(dual_rows, dual_cols, primal, row_below, row_keep):
    below = jnp.concatenate([primal[:, :, 1:], row_below], axis=2)
    diff_rows = (below - primal) * row_keep
    diff_cols = jnp.pad(primal[..., 1:] - primal[..., :-1], ((0, 0), (0, 0), (0, 0), (0, 1)))
    new_rows = dual_rows + DUAL_STEP / TV_WEIGHT * diff_rows
    new_cols = dual_cols + DUAL_STEP / TV_WEIGHT * diff_cols
    shrink = jnp.maximum(1.0, jnp.sqrt(new_rows * new_rows + new_cols * new_cols))
    return (new_rows / shrink, new_cols / shrink)

def reference(object_slices, probe_wave, propagator, offsets, adjoint):
    overhang = PR - STRIDE
    matrix = dense_matrix(propagator)
    object32 = object_slices.astype(jnp.float32)
    padded = jnp.concatenate([object32, jnp.zeros((2, SLICES, overhang, NC), jnp.float32)], axis=2)
    probe32 = probe_wave.astype(jnp.float32)
    zero_index = jnp.zeros((), jnp.int32)

    def tile_work(tile_index):
        extended = lax.dynamic_slice(padded, (zero_index, zero_index, tile_index * ROWS, zero_index), (2, SLICES, ROWS + overhang, NC))
        summed = jnp.zeros((2, SLICES, ROWS + overhang, NC), jnp.float32)
        for scan_index in range(N_SCAN):

            def add_window(position, totals):
                column = (scan_index * POS_DEV + position).astype(jnp.int32)
                offset = offsets[tile_index, column].astype(jnp.int32)
                start = (zero_index, zero_index, offset, zero_index)
                patch = lax.dynamic_slice(extended, start, (2, SLICES, PR, NC))
                exit_adjoint = adjoint[:, tile_index, column].astype(jnp.float32)
                update = window_gradient(patch, probe32, exit_adjoint, matrix)
                current = lax.dynamic_slice(totals, start, (2, SLICES, PR, NC))
                return lax.dynamic_update_slice(totals, current + update, start)
            totals = lax.fori_loop(jnp.int32(0), jnp.int32(POS_DEV), add_window, jnp.zeros_like(summed))
            summed = summed + to_bfloat(totals)
        return summed
    per_tile = lax.map(tile_work, jnp.arange(TILES, dtype=jnp.int32))
    main = per_tile[:, :, :, :ROWS]
    spill = per_tile[:, :, :, ROWS:]
    incoming = jnp.concatenate([jnp.zeros_like(spill[:1]), spill[:-1]], axis=0)
    main = main.at[:, :, :, :overhang].add(incoming)
    gradient = jnp.transpose(main, (1, 2, 0, 3, 4)).reshape(2, SLICES, NR, NC)
    target = object32 - STEP_SIZE * gradient
    row_keep = (jnp.arange(NR) < NR - 1).astype(jnp.float32).reshape(1, 1, NR, 1)
    empty_row = jnp.zeros((2, SLICES, 1, NC), jnp.float32)
    dual_rows = jnp.zeros_like(target)
    dual_cols = jnp.zeros_like(target)
    for sweep in range(TV_ITERS):
        primal = target + TV_WEIGHT * divergence(dual_rows, dual_cols, empty_row)
        dual_rows, dual_cols = dual_update(dual_rows, dual_cols, primal, empty_row, row_keep)
    return target + TV_WEIGHT * divergence(dual_rows, dual_cols, empty_row)
```

```python
import jax
import jax.numpy as jnp
from jax import lax
from jax.experimental import pallas as pl
from jax.experimental.pallas import tpu as pltpu
from jax.sharding import PartitionSpec as P

STRIDE = 16
TV_ITERS = 6
STEP_SIZE = 0.5
TV_WEIGHT = 1.0
DUAL_STEP = 0.125

F32 = jnp.float32
BF16 = jnp.bfloat16
LANES = 128
GROUP = 8
VMEM_LIMIT = 32 * 1024 * 1024


def passed_along(value, axis, steps):
    count = lax.axis_size(axis)
    leading, last = (max(0, -steps), min(count, count - steps))
    return lax.ppermute(value, axis, [(source, source + steps) for source in range(leading, last)])


def whole(memory=pltpu.VMEM):
    return pl.BlockSpec(memory_space=memory)


def cost(flops, bytes_accessed):
    return pl.CostEstimate(flops=flops, bytes_accessed=bytes_accessed, transcendentals=0)


def half_of(block, odd):
    return jnp.where(odd, block[GROUP:], block[:GROUP])


def stage(object_slices, offsets, adjoint, layers, rows, columns):
    groups = rows // GROUP

    def kernel(offset_ref, adjoint_ref, object_ref, send_ref, rows_ref, top_ref, block, edge, sems):
        scan = lax.axis_index("scan")
        start = pl.multiple_of((scan // 2) * 16, 16)
        copies = [
            pltpu.make_async_copy(object_ref.at[:, :, pl.ds(start, 16), :], block, sems.at[0]),
            pltpu.make_async_copy(object_ref.at[:, scan, pl.ds(0, 16), :], edge.at[0], sems.at[1]),
            pltpu.make_async_copy(
                object_ref.at[:, scan, pl.ds(rows - 16, 16), :], edge.at[1], sems.at[2]
            ),
        ]
        for copy in copies:
            copy.start()
        offset = offset_ref[0, 0]
        steps = offset // STRIDE
        flag = jnp.full((16, LANES), offset, jnp.int32).astype(F32).astype(BF16)
        for pair in range(groups // 2):
            source = pl.multiple_of(((pair - steps + groups) % (groups // 2)) * 16, 16)
            real = adjoint_ref[0, 0, 0, pl.ds(source, 16), :].astype(F32)
            imag = adjoint_ref[1, 0, 0, pl.ds(source, 16), :].astype(F32)
            for half in range(2):
                part = slice(half * GROUP, (half + 1) * GROUP)
                send_ref[2 * pair + half, :, :columns] = jnp.concatenate(
                    [real[part], imag[part]], axis=0
                ).astype(BF16)
                send_ref[2 * pair + half, :, columns:] = flag
        for copy in copies:
            copy.wait()
        odd = scan % 2 == 1
        for layer in range(layers):
            rows_ref[layer] = jnp.concatenate(
                [half_of(block[0, layer].astype(F32), odd), half_of(block[1, layer].astype(F32), odd)],
                axis=0,
            ).astype(BF16)
        rows_ref[layers] = jnp.concatenate(
            [edge[0, 0].astype(F32)[:GROUP], edge[0, 1].astype(F32)[:GROUP]], axis=0
        ).astype(BF16)
        top_ref[...] = jnp.concatenate(
            [edge[1, 0].astype(F32)[GROUP:], edge[1, 1].astype(F32)[GROUP:]], axis=0
        ).astype(BF16)

    return pl.pallas_call(
        kernel,
        out_shape=(
            jax.ShapeDtypeStruct((groups, 16, columns + LANES), BF16),
            jax.ShapeDtypeStruct((layers + 1, 16, columns), BF16),
            jax.ShapeDtypeStruct((16, columns), BF16),
        ),
        in_specs=[whole(pltpu.SMEM), whole(), whole(pl.ANY)],
        out_specs=(whole(), whole(), whole()),
        scratch_shapes=[
            pltpu.VMEM((2, layers, 16, columns), BF16),
            pltpu.VMEM((2, 2, 16, columns), BF16),
            pltpu.SemaphoreType.DMA((3,)),
        ],
        compiler_params=pltpu.CompilerParams(vmem_limit_bytes=VMEM_LIMIT),
        cost_estimate=cost(0, 2 * 1024 * 1024),
        name="stage",
    )(offsets, adjoint, object_slices)


def object_of(own, following, layer, block, is_own, classes):
    lanes = slice(block * LANES, (block + 1) * LANES)
    mine = own[layer, :, lanes].astype(F32)
    other = following[layer, :, lanes].astype(F32)
    picked = [jnp.where(is_own[step], mine, other) for step in range(classes)]
    real = jnp.stack([value[:GROUP] for value in picked])
    imag = jnp.stack([value[GROUP:] for value in picked])
    return real, imag


def banded(padded_ref, weights_ref, height, band):
    windows = jnp.concatenate(
        [padded_ref[pl.ds(step * 32, height), :] for step in range(band)], axis=1
    )
    return jnp.dot(windows, weights_ref[...], preferred_element_type=F32)


def forward(own_rows, next_rows, probe_wave, propagator, classes):
    layers = own_rows.shape[0] - 1
    columns = own_rows.shape[2]
    window_rows = probe_wave.shape[1]
    band = propagator.shape[1]
    blocks = columns // LANES
    centre = band // 2
    tall = classes * GROUP
    height = blocks * tall

    def kernel(own, following, probe, prop, waves, back_weights, weights, padded):
        scan = lax.axis_index("scan")
        odd = scan % 2 == 1
        is_own = [scan >= 2 * step for step in range(classes)]
        for step in range(band):
            real, imag = prop[0, step].astype(F32), prop[1, step].astype(F32)
            top = step * 2 * LANES
            weights[top : top + LANES, :LANES] = real.astype(BF16)
            weights[top : top + LANES, LANES:] = imag.astype(BF16)
            weights[top + LANES : top + 2 * LANES, :LANES] = (-imag).astype(BF16)
            weights[top + LANES : top + 2 * LANES, LANES:] = real.astype(BF16)
        padded[: centre * tall, :] = jnp.zeros((centre * tall, 2 * LANES), BF16)
        padded[(centre + blocks) * tall :, :] = jnp.zeros(
            ((band - 1 - centre) * tall, 2 * LANES), BF16
        )
        real_rows, imag_rows = [], []
        for step in range(classes):
            place = (scan - 2 * step + window_rows) % (window_rows // GROUP)
            start = pl.multiple_of((place // 2) * 16, 16)
            real_rows.append(half_of(probe[0, pl.ds(start, 16), :].astype(F32), odd))
            imag_rows.append(half_of(probe[1, pl.ds(start, 16), :].astype(F32), odd))
        real_rows = jnp.concatenate(real_rows, axis=0).astype(BF16)
        imag_rows = jnp.concatenate(imag_rows, axis=0).astype(BF16)
        for block in range(blocks):
            lanes = slice(block * LANES, (block + 1) * LANES)
            waves[0, block * tall : (block + 1) * tall, :LANES] = real_rows[:, lanes]
            waves[0, block * tall : (block + 1) * tall, LANES:] = imag_rows[:, lanes]

        def layer_step(layer, carry):
            for block in range(blocks):
                at = slice(block * tall, (block + 1) * tall)
                wave_real = waves[layer, at, :LANES].astype(F32).reshape(classes, GROUP, LANES)
                wave_imag = waves[layer, at, LANES:].astype(F32).reshape(classes, GROUP, LANES)
                obj_real, obj_imag = object_of(own, following, layer, block, is_own, classes)
                real = obj_real * wave_real - obj_imag * wave_imag
                imag = obj_real * wave_imag + obj_imag * wave_real
                at = slice((block + centre) * tall, (block + centre + 1) * tall)
                padded[at, :LANES] = real.reshape(tall, LANES).astype(BF16)
                padded[at, LANES:] = imag.reshape(tall, LANES).astype(BF16)
            waves[layer + 1] = banded(padded, weights, height, band).astype(BF16)
            return carry

        lax.fori_loop(0, layers - 1, layer_step, 0)
        for step in range(band):
            real, imag = prop[0, step].astype(F32).T, prop[1, step].astype(F32).T
            top = (band - 1 - step) * 2 * LANES
            back_weights[top : top + LANES, :LANES] = real.astype(BF16)
            back_weights[top : top + LANES, LANES:] = (-imag).astype(BF16)
            back_weights[top + LANES : top + 2 * LANES, :LANES] = imag.astype(BF16)
            back_weights[top + LANES : top + 2 * LANES, LANES:] = real.astype(BF16)

    flops = (layers - 1) * 2 * height * band * 4 * LANES * LANES
    return pl.pallas_call(
        kernel,
        out_shape=(
            jax.ShapeDtypeStruct((layers, height, 2 * LANES), BF16),
            jax.ShapeDtypeStruct((band * 2 * LANES, 2 * LANES), BF16),
        ),
        in_specs=[whole()] * 4,
        out_specs=(whole(), whole()),
        scratch_shapes=[
            pltpu.VMEM((band * 2 * LANES, 2 * LANES), BF16),
            pltpu.VMEM(((blocks + band - 1) * tall, 2 * LANES), BF16),
        ],
        compiler_params=pltpu.CompilerParams(vmem_limit_bytes=VMEM_LIMIT),
        cost_estimate=cost(flops, 4 * 1024 * 1024),
        name="forward",
    )(own_rows, next_rows, probe_wave, propagator)


def backward(received, waves, own_rows, next_rows, back_weights, classes):
    layers = own_rows.shape[0] - 1
    columns = own_rows.shape[2]
    positions = received.shape[0]
    blocks = columns // LANES
    band = back_weights.shape[0] // (2 * LANES)
    before_count = band - 1 - band // 2
    tall = classes * GROUP
    height = blocks * tall

    def kernel(received, waves, own, following, weights, out, padded, fields):
        scan = lax.axis_index("scan")
        is_own = [scan >= 2 * step for step in range(classes)]
        padded[: before_count * tall, :] = jnp.zeros((before_count * tall, 2 * LANES), BF16)
        padded[(before_count + blocks) * tall :, :] = jnp.zeros(
            ((band - 1 - before_count) * tall, 2 * LANES), BF16
        )
        flags = [received[place, :, columns:].astype(F32) for place in range(positions)]
        for block in range(blocks):
            lanes = slice(block * LANES, (block + 1) * LANES)
            values = [received[place, :, lanes].astype(F32) for place in range(positions)]
            sums = []
            for step in range(classes):
                picked = [
                    jnp.where(flag == float(step * STRIDE), value, 0.0)
                    for flag, value in zip(flags, values)
                ]
                while len(picked) > 1:
                    picked = [
                        sum(picked[place : place + 2][1:], picked[place])
                        for place in range(0, len(picked), 2)
                    ]
                sums.append(picked[0])
            at = slice((block + before_count) * tall, (block + before_count + 1) * tall)
            padded[at, :LANES] = jnp.concatenate([s[:GROUP] for s in sums], axis=0).astype(BF16)
            padded[at, LANES:] = jnp.concatenate([s[GROUP:] for s in sums], axis=0).astype(BF16)

        def layer_step(index, carry):
            layer = layers - 1 - index
            fields[...] = banded(padded, weights, height, band)
            for block in range(blocks):
                at = slice(block * tall, (block + 1) * tall)
                lanes = slice(block * LANES, (block + 1) * LANES)
                real = fields[at, :LANES].reshape(classes, GROUP, LANES)
                imag = fields[at, LANES:].reshape(classes, GROUP, LANES)
                wave_real = waves[layer, at, :LANES].astype(F32).reshape(classes, GROUP, LANES)
                wave_imag = waves[layer, at, LANES:].astype(F32).reshape(classes, GROUP, LANES)
                term_real = real * wave_real + imag * wave_imag
                term_imag = imag * wave_real - real * wave_imag
                kept = [jnp.zeros((GROUP, LANES), F32)] * 2
                sent = [jnp.zeros((GROUP, LANES), F32)] * 2
                for step in range(classes):
                    for part, term in enumerate((term_real[step], term_imag[step])):
                        kept[part] = kept[part] + jnp.where(is_own[step], term, 0.0)
                        sent[part] = sent[part] + jnp.where(is_own[step], 0.0, term)
                out[layer, :, lanes] = jnp.concatenate(kept + sent, axis=0).astype(BF16)
                obj_real, obj_imag = object_of(own, following, layer, block, is_own, classes)
                up_real = real * obj_real + imag * obj_imag
                up_imag = imag * obj_real - real * obj_imag
                at = slice((block + before_count) * tall, (block + before_count + 1) * tall)
                padded[at, :LANES] = up_real.reshape(tall, LANES).astype(BF16)
                padded[at, LANES:] = up_imag.reshape(tall, LANES).astype(BF16)
            return carry

        lax.fori_loop(0, layers, layer_step, 0)

    flops = layers * 2 * height * band * 4 * LANES * LANES
    return pl.pallas_call(
        kernel,
        out_shape=jax.ShapeDtypeStruct((layers, 4 * GROUP, columns), BF16),
        in_specs=[whole()] * 5,
        out_specs=whole(),
        scratch_shapes=[
            pltpu.VMEM(((blocks + band - 1) * tall, 2 * LANES), BF16),
            pltpu.VMEM((height, 2 * LANES), F32),
        ],
        compiler_params=pltpu.CompilerParams(vmem_limit_bytes=VMEM_LIMIT),
        cost_estimate=cost(flops, 4 * 1024 * 1024),
        name="backward",
    )(received, waves, own_rows, next_rows, back_weights)


def denoise(object_slices, gradient, from_above, from_below, edge_above, edge_below):
    rows, columns = object_slices.shape[2:]
    groups = rows // GROUP
    spilled = from_above.shape[0] - 1
    span = rows + 2 * GROUP
    tiles = lax.axis_size("tile")

    def kernel(object_ref, grad, above, below, top, bottom, out, slab, target, primal, drows, dcols, sem):
        scan, tile = lax.axis_index("scan"), lax.axis_index("tile")
        copy = pltpu.make_async_copy(object_ref.at[:, scan], slab, sem)
        copy.start()
        copy.wait()
        for part in range(2):
            piece = slice(part * GROUP, (part + 1) * GROUP)
            spill = slice((part + 2) * GROUP, (part + 3) * GROUP)
            target[part, :GROUP] = top[...].astype(F32)[piece] - STEP_SIZE * above[spilled].astype(
                F32
            )[piece]
            for group in range(groups):
                slope = grad[group].astype(F32)[piece]
                if group < spilled:
                    slope = slope + above[group].astype(F32)[piece]
                pair = slab[part, (group // 2) * 16 : (group // 2) * 16 + 16].astype(F32)
                half = pair[(group % 2) * GROUP : (group % 2 + 1) * GROUP]
                target[part, (group + 1) * GROUP : (group + 2) * GROUP] = half - STEP_SIZE * slope
            target[part, (groups + 1) * GROUP :] = bottom[0].astype(F32)[piece] - STEP_SIZE * (
                below[...].astype(F32)[piece] + grad[0].astype(F32)[spill]
            )
        column = lax.broadcasted_iota(jnp.int32, (GROUP, columns), 1)
        first, last = column == 0, column == columns - 1
        row = lax.broadcasted_iota(jnp.int32, (GROUP, columns), 0)
        first_row, last_row = tile * rows, tiles * rows - 1

        def shifted_right(value):
            return jnp.where(first, 0.0, pltpu.roll(value, 1, 1))

        def above_of(ref, part, group):
            value = ref[part, group * GROUP : (group + 1) * GROUP]
            lead = ref[part, (group - 1) * GROUP : group * GROUP] if group else jnp.zeros_like(value)
            return jnp.where(row == 0, pltpu.roll(lead, 1, 0), pltpu.roll(value, 1, 0))

        def below_of(ref, part, group):
            value = ref[part, group * GROUP : (group + 1) * GROUP]
            if group + 1 < span // GROUP:
                after = ref[part, (group + 1) * GROUP : (group + 2) * GROUP]
            else:
                after = value
            return jnp.where(
                row == GROUP - 1, pltpu.roll(after, GROUP - 1, 0), pltpu.roll(value, GROUP - 1, 0)
            )

        def primal_of(part, group):
            at = slice(group * GROUP, (group + 1) * GROUP)
            rows_dual, cols_dual = drows[part, at], dcols[part, at]
            diverged = (rows_dual - above_of(drows, part, group)) + (
                cols_dual - shifted_right(cols_dual)
            )
            return target[part, at] + TV_WEIGHT * diverged

        drows[...] = jnp.zeros(drows.shape, F32)
        dcols[...] = jnp.zeros(dcols.shape, F32)

        def sweep(_, carry):
            for part in range(2):
                for group in range(span // GROUP):
                    primal[part, group * GROUP : (group + 1) * GROUP] = primal_of(part, group)
                for group in range(span // GROUP):
                    at = slice(group * GROUP, (group + 1) * GROUP)
                    value = primal[part, at]
                    place = first_row + (group - 1) * GROUP + row
                    keep = (place >= 0) & (place < last_row)
                    diff_rows = jnp.where(keep, below_of(primal, part, group) - value, 0.0)
                    diff_cols = jnp.where(last, 0.0, pltpu.roll(value, columns - 1, 1) - value)
                    new_rows = drows[part, at] + DUAL_STEP / TV_WEIGHT * diff_rows
                    new_cols = dcols[part, at] + DUAL_STEP / TV_WEIGHT * diff_cols
                    scale = jnp.minimum(1.0, lax.rsqrt(new_rows * new_rows + new_cols * new_cols))
                    drows[part, at] = new_rows * scale
                    dcols[part, at] = new_cols * scale
            return carry

        lax.fori_loop(0, TV_ITERS, sweep, 0)
        for part in range(2):
            for group in range(groups):
                out[part, 0, group * GROUP : (group + 1) * GROUP] = primal_of(part, group + 1)

    buffer = pltpu.VMEM((2, span, columns), F32)
    return pl.pallas_call(
        kernel,
        out_shape=jax.ShapeDtypeStruct((2, 1, rows, columns), F32),
        grid=(1,),
        in_specs=[
            whole(pl.ANY),
            whole(),
            whole(),
            whole(),
            whole(),
            pl.BlockSpec((1,) + edge_below.shape[1:], lambda _: (edge_below.shape[0] - 1, 0, 0)),
        ],
        out_specs=whole(),
        scratch_shapes=[
            pltpu.VMEM((2, rows, columns), BF16),
            buffer,
            buffer,
            buffer,
            buffer,
            pltpu.SemaphoreType.DMA,
        ],
        compiler_params=pltpu.CompilerParams(vmem_limit_bytes=VMEM_LIMIT),
        cost_estimate=cost(0, 4 * 1024 * 1024),
        name="denoise",
    )(object_slices, gradient, from_above, from_below, edge_above, edge_below)


def per_device(object_slices, probe_wave, propagator, offsets, adjoint):
    layers, rows, columns = object_slices.shape[1:]
    window_rows = probe_wave.shape[1]
    classes = window_rows // STRIDE
    spilled = (window_rows - STRIDE) // GROUP
    send, own_rows, top = stage(object_slices, offsets, adjoint, layers, rows, columns)
    next_rows = passed_along(own_rows, "tile", -1)
    edge_above = passed_along(top, "tile", 1)
    received = lax.all_to_all(send, "scan", 0, 0, tiled=True)
    waves, back_weights = forward(own_rows, next_rows, probe_wave, propagator, classes)
    chunks = backward(received, waves, own_rows, next_rows, back_weights, classes)
    gradient = lax.all_to_all(chunks, "scan", 0, 0, tiled=True)
    upward = jnp.concatenate(
        [gradient[:spilled, 2 * GROUP :], gradient[rows // GROUP - 1 :, : 2 * GROUP]], axis=0
    )
    from_above = passed_along(upward, "tile", 1)
    from_below = passed_along(gradient[0, : 2 * GROUP], "tile", -1)
    return denoise(object_slices, gradient, from_above, from_below, edge_above, next_rows)


def solution(mesh):
    in_specs = (
        P(None, None, "tile", None),
        P(),
        P(),
        P("tile", "scan"),
        P(None, "tile", "scan", None, None),
    )
    out_specs = P(None, "scan", "tile", None)
    return jax.shard_map(
        per_device, mesh=mesh, in_specs=in_specs, out_specs=out_specs, check_vma=False
    )
```

```python
import jax
import jax.numpy as jnp
from jax import lax
from jax.experimental import pallas as pl
from jax.experimental.pallas import tpu as pltpu
from jax.sharding import PartitionSpec as P

STRIDE = 16
TV_ITERS = 6
STEP_SIZE = 0.5
TV_WEIGHT = 1.0
DUAL_STEP = 0.125

F32 = jnp.float32
BF16 = jnp.bfloat16
LANES = 128
GROUP = 8
VMEM_LIMIT = 32 * 1024 * 1024
PICK_LIMIT = 52 * 1024 * 1024


def passed_along(value, axis, steps):
    count = lax.axis_size(axis)
    leading, last = (max(0, -steps), min(count, count - steps))
    return lax.ppermute(value, axis, [(source, source + steps) for source in range(leading, last)])


def swapped(value, first):
    pairs = [(place, place + 1) for place in range(first, lax.axis_size("tile") - 1, 2)]
    return lax.ppermute(value, "tile", pairs + [(other, one) for one, other in pairs])


def whole(memory=pltpu.VMEM):
    return pl.BlockSpec(memory_space=memory)


def cost(flops, bytes_accessed):
    return pl.CostEstimate(flops=flops, bytes_accessed=bytes_accessed, transcendentals=0)


def half_of(block, odd):
    return jnp.where(odd, block[GROUP:], block[:GROUP])


def spread(offsets, adjoint):
    rows, columns = adjoint.shape[3:]
    groups = rows // GROUP
    pairs = groups // 2

    def kernel(offset_ref, field, send):
        offset = offset_ref[0, 0]
        steps = offset // STRIDE
        flag = jnp.full((16, LANES), offset, jnp.int32).astype(F32).astype(BF16)
        for pair in range(pairs):
            source = pl.multiple_of(((pair - steps + pairs) % pairs) * 16, 16)
            real = field[0, 0, 0, pl.ds(source, 16), :].astype(F32)
            imag = field[1, 0, 0, pl.ds(source, 16), :].astype(F32)
            for half in range(2):
                part = slice(half * GROUP, (half + 1) * GROUP)
                send[2 * pair + half, :, :columns] = jnp.concatenate(
                    [real[part], imag[part]], axis=0
                ).astype(BF16)
                send[2 * pair + half, :, columns:] = flag

    return pl.pallas_call(
        kernel,
        out_shape=jax.ShapeDtypeStruct((groups, 16, columns + LANES), BF16),
        in_specs=[whole(pltpu.SMEM), whole()],
        out_specs=whole(),
        compiler_params=pltpu.CompilerParams(vmem_limit_bytes=VMEM_LIMIT),
        cost_estimate=cost(0, 512 * 1024),
        name="spread",
    )(offsets, adjoint)


def pick(object_slices, after):
    layers, rows, columns = object_slices.shape[1:]

    def kernel(object_hbm, _, own_rows, edges, slab, block, sems):
        scan = lax.axis_index("scan")
        start = pl.multiple_of((scan // 2) * 16, 16)
        copies = [
            pltpu.make_async_copy(object_hbm.at[:, :, pl.ds(start, 16), :], block, sems.at[0]),
            pltpu.make_async_copy(object_hbm.at[:, scan], slab, sems.at[1]),
        ]
        for copy in copies:
            copy.start()
        for copy in copies:
            copy.wait()
        odd = scan % 2 == 1
        for layer in range(layers):
            own_rows[layer] = jnp.concatenate(
                [half_of(block[part, layer].astype(F32), odd) for part in range(2)], axis=0
            ).astype(BF16)
        edges[0] = jnp.concatenate(
            [slab[part, rows - 16 :].astype(F32)[GROUP:] for part in range(2)], axis=0
        ).astype(BF16)
        edges[1] = jnp.concatenate(
            [slab[part, :16].astype(F32)[:GROUP] for part in range(2)], axis=0
        ).astype(BF16)

    return pl.pallas_call(
        kernel,
        out_shape=(
            jax.ShapeDtypeStruct((layers, 16, columns), BF16),
            jax.ShapeDtypeStruct((2, 16, columns), BF16),
            jax.ShapeDtypeStruct((2, rows, columns), BF16),
        ),
        in_specs=[whole(pltpu.HBM), whole(pl.ANY)],
        out_specs=(whole(),) * 3,
        scratch_shapes=[
            pltpu.VMEM((2, layers, 16, columns), BF16),
            pltpu.SemaphoreType.DMA((2,)),
        ],
        compiler_params=pltpu.CompilerParams(vmem_limit_bytes=PICK_LIMIT),
        cost_estimate=cost(0, 2 * 1024 * 1024),
        name="pick",
    )(object_slices, after)


def sum_by_offset(received, after, classes):
    positions, _, width = received.shape
    columns = width - LANES

    def kernel(received, _, first, others):
        flags = [received[place, :, columns:].astype(F32) for place in range(positions)]
        for block in range(columns // LANES):
            lanes = slice(block * LANES, (block + 1) * LANES)
            values = [received[place, :, lanes].astype(F32) for place in range(positions)]
            for step in range(classes):
                picked = [
                    jnp.where(flag == float(step * STRIDE), value, 0.0)
                    for flag, value in zip(flags, values)
                ]
                while len(picked) > 1:
                    picked = [sum(picked[k + 1 : k + 2], picked[k]) for k in range(0, len(picked), 2)]
                if step == 0:
                    first[:, lanes] = picked[0].astype(BF16)
                else:
                    others[step - 1, :, lanes] = picked[0].astype(BF16)

    return pl.pallas_call(
        kernel,
        out_shape=(
            jax.ShapeDtypeStruct((16, columns), BF16),
            jax.ShapeDtypeStruct((classes - 1, 16, columns), BF16),
        ),
        in_specs=[whole(), whole(pl.ANY)],
        out_specs=(whole(), whole()),
        compiler_params=pltpu.CompilerParams(vmem_limit_bytes=VMEM_LIMIT),
        cost_estimate=cost(1, 1),
        name="sum_by_offset",
    )(received, after)


def object_of(own, layer, block):
    value = own[layer, :, block * LANES : (block + 1) * LANES].astype(F32)
    real, imag = value[:GROUP], value[GROUP:]
    return jnp.concatenate([real, real], axis=0), jnp.concatenate([imag, imag], axis=0)


def windows_of(padded, height, band):
    return jnp.concatenate([padded[pl.ds(step * 16, height), :] for step in range(band)], axis=1)


def forward(own_rows, probe_wave, propagator, classes):
    layers = own_rows.shape[0]
    columns = own_rows.shape[2]
    window_rows = probe_wave.shape[1]
    band = propagator.shape[1]
    blocks = columns // LANES
    centre = band // 2
    halves = classes // 2
    height = blocks * 16

    def kernel(own, probe, prop, waves, weights, padded_one, padded_two):
        padded = (padded_one, padded_two)
        scan = lax.axis_index("scan")
        odd = scan % 2 == 1
        for step in range(band):
            real, imag = prop[0, step], prop[1, step]
            top = step * 2 * LANES
            weights[top : top + LANES, :LANES] = real
            weights[top : top + LANES, LANES:] = imag
            weights[top + LANES : top + 2 * LANES, :LANES] = -imag
            weights[top + LANES : top + 2 * LANES, LANES:] = real
        for half in range(halves):
            padded[half][: centre * 16, :] = jnp.zeros((centre * 16, 2 * LANES), BF16)
            padded[half][(centre + blocks) * 16 :, :] = jnp.zeros(
                ((band - 1 - centre) * 16, 2 * LANES), BF16
            )
            for part in range(2):
                found = []
                for step in (2 * half, 2 * half + 1):
                    place = (scan - 2 * step + window_rows) % (window_rows // GROUP)
                    start = pl.multiple_of((place // 2) * 16, 16)
                    found.append(half_of(probe[part, pl.ds(start, 16), :].astype(F32), odd))
                found = jnp.concatenate(found, axis=0).astype(BF16)
                for block in range(blocks):
                    waves[0, half, block * 16 : (block + 1) * 16, part * LANES : (part + 1) * LANES] = (
                        found[:, block * LANES : (block + 1) * LANES]
                    )

        def transmit(layer, half):
            for block in range(blocks):
                at = slice(block * 16, (block + 1) * 16)
                wave_real = waves[layer, half, at, :LANES].astype(F32)
                wave_imag = waves[layer, half, at, LANES:].astype(F32)
                obj_real, obj_imag = object_of(own, layer, block)
                at = slice((block + centre) * 16, (block + centre + 1) * 16)
                padded[half][at, :LANES] = (obj_real * wave_real - obj_imag * wave_imag).astype(BF16)
                padded[half][at, LANES:] = (obj_real * wave_imag + obj_imag * wave_real).astype(BF16)

        def propagate(layer, half):
            field = jnp.dot(
                windows_of(padded[half], height, band), weights[...], preferred_element_type=F32
            )
            waves[layer + 1, half] = field.astype(BF16)

        transmit(0, 0)

        def layer_step(layer, carry):
            propagate(layer, 0)
            transmit(layer, 1)
            propagate(layer, 1)
            transmit(layer + 1, 0)
            return carry

        for layer in range(layers - 1):
            layer_step(layer, 0)

    flops = (layers - 1) * 4 * height * band * 4 * LANES * LANES
    padded = pltpu.VMEM(((blocks + band - 1) * 16, 2 * LANES), BF16)
    return pl.pallas_call(
        kernel,
        out_shape=jax.ShapeDtypeStruct((layers, halves, height, 2 * LANES), BF16),
        in_specs=[whole()] * 3,
        out_specs=whole(),
        scratch_shapes=[pltpu.VMEM((band * 2 * LANES, 2 * LANES), BF16), padded, padded],
        compiler_params=pltpu.CompilerParams(vmem_limit_bytes=VMEM_LIMIT),
        cost_estimate=cost(flops, 4 * 1024 * 1024),
        name="forward",
    )(own_rows, probe_wave, propagator)


def backward(first, others, incoming, waves, own_rows, propagator, classes):
    layers = own_rows.shape[0]
    columns = own_rows.shape[2]
    blocks = columns // LANES
    band = propagator.shape[1]
    lead = band - 1 - band // 2
    halves = classes // 2
    height = blocks * 16

    def kernel(first, others, incoming, waves, own, prop, out, weights, padded_one, padded_two, fields, terms):
        padded = (padded_one, padded_two)
        scan = lax.axis_index("scan")
        is_own = [scan >= 2 * step for step in range(classes)]
        for step in range(band):
            real, imag = prop[0, step], prop[1, step]
            real, imag = real.T, imag.T
            top = (band - 1 - step) * 2 * LANES
            weights[top : top + LANES, :LANES] = real
            weights[top : top + LANES, LANES:] = -imag
            weights[top + LANES : top + 2 * LANES, :LANES] = imag
            weights[top + LANES : top + 2 * LANES, LANES:] = real
        for half in range(halves):
            padded[half][: lead * 16, :] = jnp.zeros((lead * 16, 2 * LANES), BF16)
            padded[half][(lead + blocks) * 16 :, :] = jnp.zeros(
                ((band - 1 - lead) * 16, 2 * LANES), BF16
            )
        for block in range(blocks):
            lanes = slice(block * LANES, (block + 1) * LANES)
            sums = [first[:, lanes].astype(F32)]
            for step in range(classes - 1):
                mine, other = others[step, :, lanes], incoming[step, :, lanes]
                sums.append(jnp.where(is_own[step + 1], mine, other).astype(F32))
            at = slice((block + lead) * 16, (block + lead + 1) * 16)
            for half in range(halves):
                pair = sums[2 * half : 2 * half + 2]
                padded[half][at, :LANES] = jnp.concatenate([s[:GROUP] for s in pair], axis=0).astype(BF16)
                padded[half][at, LANES:] = jnp.concatenate([s[GROUP:] for s in pair], axis=0).astype(BF16)

        def propagate(half):
            return jnp.dot(
                windows_of(padded[half], height, band), weights[...], preferred_element_type=F32
            )

        def meet(layer, half, field):
            for block in range(blocks):
                at = slice(block * 16, (block + 1) * 16)
                lanes = slice(block * LANES, (block + 1) * LANES)
                real, imag = field[at, :LANES], field[at, LANES:]
                wave_real = waves[layer, half, at, :LANES].astype(F32)
                wave_imag = waves[layer, half, at, LANES:].astype(F32)
                both = (
                    real * wave_real + imag * wave_imag,
                    imag * wave_real - real * wave_imag,
                )
                total = jnp.concatenate([term[:GROUP] + term[GROUP:] for term in both], axis=0)
                if half == 0:
                    terms[:, lanes] = total
                else:
                    out[layer, :, lanes] = (terms[:, lanes] + total).astype(BF16)
                obj_real, obj_imag = object_of(own, layer, block)
                at = slice((block + lead) * 16, (block + lead + 1) * 16)
                padded[half][at, :LANES] = (real * obj_real + imag * obj_imag).astype(BF16)
                padded[half][at, LANES:] = (imag * obj_real - real * obj_imag).astype(BF16)

        fields[...] = propagate(0)

        def layer_step(index, carry):
            layer = layers - 1 - index
            second = propagate(1)
            meet(layer, 0, fields)
            fields[...] = propagate(0)
            meet(layer, 1, second)
            return carry

        for index in range(layers):
            layer_step(index, 0)

    flops = layers * 4 * height * band * 4 * LANES * LANES
    padded = pltpu.VMEM(((blocks + band - 1) * 16, 2 * LANES), BF16)
    return pl.pallas_call(
        kernel,
        out_shape=jax.ShapeDtypeStruct((layers, 2 * GROUP, columns), BF16),
        in_specs=[whole()] * 6,
        out_specs=whole(),
        scratch_shapes=[
            pltpu.VMEM((band * 2 * LANES, 2 * LANES), BF16),
            padded,
            padded,
            pltpu.VMEM((height, 2 * LANES), F32),
            pltpu.VMEM((2 * GROUP, columns), F32),
        ],
        compiler_params=pltpu.CompilerParams(vmem_limit_bytes=VMEM_LIMIT),
        cost_estimate=cost(flops, 4 * 1024 * 1024),
        name="backward",
    )(first, others, incoming, waves, own_rows, propagator)


def denoise(slab, gradient, from_even, from_odd):
    rows, columns = slab.shape[1:]
    groups = rows // GROUP
    span = groups + 2
    blocks = columns // LANES
    tiles = lax.axis_size("tile")
    scale = DUAL_STEP / TV_WEIGHT
    above_at = divmod(GROUP - 1, span)
    last_at = divmod(GROUP + rows - 1, span)

    def kernel(slab, grad, even, odd, out, plain, target, rows_one, cols_one, rows_two, cols_two, primal):
        tile = lax.axis_index("tile")
        is_odd = tile % 2 == 1

        def above(place, piece):
            return jnp.where(is_odd, even[place], odd[place]).astype(F32)[piece]

        def below(place, piece):
            return jnp.where(is_odd, odd[place], even[place]).astype(F32)[piece]

        lane = lax.broadcasted_iota(jnp.int32, (GROUP, LANES), 1)
        row = lax.broadcasted_iota(jnp.int32, (GROUP, LANES), 0)
        first, last = lane == 0, lane == LANES - 1
        zero = jnp.zeros((GROUP, LANES), F32)
        one, two = (rows_one, cols_one), (rows_two, cols_two)
        no_top = (row == above_at[0]) & (tile == 0)
        no_bottom = (row == last_at[0]) & (tile == tiles - 1)

        def put(part, group, image, slope):
            value = scale * (image - STEP_SIZE * slope)
            for b in range(blocks):
                lanes = slice(b * LANES, (b + 1) * LANES)
                plain[part, b, group * GROUP : (group + 1) * GROUP] = value[:, lanes]

        for part in range(2):
            piece = slice(part * GROUP, (part + 1) * GROUP)
            put(part, 0, above(1, piece), above(0, piece))
            for group in range(groups):
                pair = slab[part, (group // 2) * 16 : (group // 2) * 16 + 16].astype(F32)
                half = pair[(group % 2) * GROUP : (group % 2 + 1) * GROUP]
                put(part, group + 1, half, grad[group].astype(F32)[piece])
            put(part, groups + 1, below(3, piece), below(2, piece))

        def at(ref, part, step):
            return [ref[part, b, step] for b in range(blocks)]

        def shifted(cols):
            turned = [pltpu.roll(v, 1, 1) for v in cols]
            return [jnp.where(first, turned[b - 1] if b else zero, turned[b]) for b in range(blocks)]

        def primal_of(duals, part, step, previous):
            dual, cols, base = at(duals[0], part, step), at(duals[1], part, step), at(target, part, step)
            moved = shifted(cols)
            result = [
                base[b] + (scale * TV_WEIGHT) * ((dual[b] - previous[b]) + (cols[b] - moved[b]))
                for b in range(blocks)
            ]
            return result, dual

        def update(duals, results, part, step, value, after):
            dual, cols = at(duals[0], part, step), at(duals[1], part, step)
            turned = [pltpu.roll(v, LANES - 1, 1) for v in value]
            for b in range(blocks):
                below = after[b]
                if step == above_at[1]:
                    below = jnp.where(no_top, value[b], below)
                if step == last_at[1]:
                    below = jnp.where(no_bottom, value[b], below)
                right = jnp.where(last, turned[b + 1] if b + 1 < blocks else value[b], turned[b])
                new_rows = dual[b] + (below - value[b])
                new_cols = cols[b] + (right - value[b])
                shrink = jnp.minimum(1.0, lax.rsqrt(new_rows * new_rows + new_cols * new_cols))
                results[0][part, b, step] = new_rows * shrink
                results[1][part, b, step] = new_cols * shrink

        def before_first(duals, part):
            return [
                jnp.where(row == 0, 0.0, pltpu.roll(v, 1, 0)) for v in at(duals[0], part, span - 1)
            ]

        def sweep(duals, results, part):
            previous = before_first(duals, part)
            for step in range(span):
                value, previous = primal_of(duals, part, step, previous)
                for b in range(blocks):
                    primal[part, b, step] = value[b]
                if step == 0:
                    for b in range(blocks):
                        primal[part, b, span] = pltpu.roll(value[b], GROUP - 1, 0)
            for step in range(span):
                update(duals, results, part, step, at(primal, part, step), at(primal, part, step + 1))

        def image(part, carry):
            for step in range(span):
                for b in range(blocks):
                    target[part, b, step] = plain[part, b, pl.ds(step, GROUP, stride=span), :]
                    rows_one[part, b, step] = zero
                    cols_one[part, b, step] = zero

            def repeat(_, carry):
                sweep(one, two, part)
                sweep(two, one, part)
                return carry

            lax.fori_loop(0, TV_ITERS // 2, repeat, 0)
            dual = before_first(one, part)
            for step in range(span):
                result, dual = primal_of(one, part, step, dual)
                for b in range(blocks):
                    plain[part, b, pl.ds(step, GROUP, stride=span), :] = result[b] * (1.0 / scale)
            for b in range(blocks):
                out[part, 0, :, b * LANES : (b + 1) * LANES] = plain[part, b, GROUP : GROUP + rows]
            return carry

        image(0, 0)
        image(1, 0)

    buffer = pltpu.VMEM((2, blocks, span, GROUP, LANES), F32)
    return pl.pallas_call(
        kernel,
        out_shape=jax.ShapeDtypeStruct((2, 1, rows, columns), F32),
        in_specs=[whole()] * 4,
        out_specs=whole(),
        scratch_shapes=[
            pltpu.VMEM((2, blocks, span * GROUP, LANES), F32),
            buffer,
            buffer,
            buffer,
            buffer,
            buffer,
            pltpu.VMEM((2, blocks, span + 1, GROUP, LANES), F32),
        ],
        compiler_params=pltpu.CompilerParams(vmem_limit_bytes=VMEM_LIMIT),
        cost_estimate=cost(0, 4 * 1024 * 1024),
        name="denoise",
    )(slab, gradient, from_even, from_odd)


def per_device(object_slices, probe_wave, propagator, offsets, adjoint):
    classes = probe_wave.shape[1] // STRIDE
    send = spread(offsets, adjoint)
    received = lax.all_to_all(send, "scan", 0, 0, tiled=True)
    own_rows, edges, slab = pick(object_slices, send)
    waves = forward(own_rows, probe_wave, propagator, classes)
    first, others = sum_by_offset(received, waves, classes)
    incoming = passed_along(others, "tile", 1)
    chunks = backward(first, others, incoming, waves, own_rows, propagator, classes)
    gradient = lax.all_to_all(chunks, "scan", 0, 0, tiled=True)
    outward = jnp.concatenate([gradient[-1:], edges[:1], gradient[:1], edges[1:]], axis=0)
    return denoise(slab, gradient, swapped(outward, 0), swapped(outward, 1))


def solution(mesh):
    in_specs = (
        P(None, None, "tile", None),
        P(),
        P(),
        P("tile", "scan"),
        P(None, "tile", "scan", None, None),
    )
    out_specs = P(None, "scan", "tile", None)
    return jax.shard_map(
        per_device, mesh=mesh, in_specs=in_specs, out_specs=out_specs, check_vma=False
    )
```

```python
import jax
import jax.numpy as jnp
from jax import lax
from jax.experimental import pallas as pl
from jax.experimental.pallas import tpu as pltpu
from jax.sharding import PartitionSpec as P

STRIDE = 16
TV_ITERS = 6
STEP_SIZE = 0.5
TV_WEIGHT = 1.0
DUAL_STEP = 0.125

F32 = jnp.float32
BF16 = jnp.bfloat16
LANES = 128
GROUP = 8
VMEM_LIMIT = 32 * 1024 * 1024
PICK_LIMIT = 52 * 1024 * 1024


def passed_along(value, axis, steps):
    count = lax.axis_size(axis)
    leading, last = (max(0, -steps), min(count, count - steps))
    return lax.ppermute(value, axis, [(source, source + steps) for source in range(leading, last)])


def swapped(value, first):
    pairs = [(place, place + 1) for place in range(first, lax.axis_size("tile") - 1, 2)]
    return lax.ppermute(value, "tile", pairs + [(other, one) for one, other in pairs])


def whole(memory=pltpu.VMEM):
    return pl.BlockSpec(memory_space=memory)


def cost(flops, bytes_accessed):
    return pl.CostEstimate(flops=flops, bytes_accessed=bytes_accessed, transcendentals=0)


def half_of(block, odd):
    return jnp.where(odd, block[GROUP:], block[:GROUP])


def spread(offsets, adjoint):
    rows, columns = adjoint.shape[3:]
    groups = rows // GROUP
    pairs = groups // 2

    def kernel(field, offset_ref, send):
        offset = jnp.broadcast_to(offset_ref[...], (16, LANES))
        flag = offset.astype(F32).astype(BF16)
        steps = [
            jnp.broadcast_to(offset_ref[...], (16, columns)) == step * STRIDE for step in range(pairs)
        ]
        groups_of = [
            [field[part, 0, 0, pair * 16 : (pair + 1) * 16, :].astype(F32) for pair in range(pairs)]
            for part in range(2)
        ]
        for pair in range(pairs):
            turned = []
            for part in range(2):
                value = groups_of[part][pair]
                for step in range(1, pairs):
                    value = jnp.where(steps[step], groups_of[part][(pair - step) % pairs], value)
                turned.append(value)
            for half in range(2):
                part = slice(half * GROUP, (half + 1) * GROUP)
                send[2 * pair + half, :, :columns] = jnp.concatenate(
                    [value[part] for value in turned], axis=0
                ).astype(BF16)
                send[2 * pair + half, :, columns:] = flag

    return pl.pallas_call(
        kernel,
        out_shape=jax.ShapeDtypeStruct((groups, 16, columns + LANES), BF16),
        in_specs=[whole(), whole()],
        out_specs=whole(),
        compiler_params=pltpu.CompilerParams(vmem_limit_bytes=VMEM_LIMIT),
        cost_estimate=cost(0, 512 * 1024),
        name="spread",
    )(adjoint, offsets)


def pick(object_slices, after):
    layers, _, columns = object_slices.shape[1:]

    def kernel(object_hbm, _, own_rows, block, sem):
        scan = lax.axis_index("scan")
        start = pl.multiple_of((scan // 2) * 16, 16)
        copy = pltpu.make_async_copy(object_hbm.at[:, :, pl.ds(start, 16), :], block, sem)
        copy.start()
        copy.wait()
        odd = scan % 2 == 1
        for layer in range(layers):
            own_rows[layer] = jnp.concatenate(
                [half_of(block[part, layer].astype(F32), odd) for part in range(2)], axis=0
            ).astype(BF16)

    return pl.pallas_call(
        kernel,
        out_shape=jax.ShapeDtypeStruct((layers, 16, columns), BF16),
        in_specs=[whole(pltpu.HBM), whole(pl.ANY)],
        out_specs=whole(),
        scratch_shapes=[pltpu.VMEM((2, layers, 16, columns), BF16), pltpu.SemaphoreType.DMA],
        compiler_params=pltpu.CompilerParams(vmem_limit_bytes=PICK_LIMIT),
        cost_estimate=cost(0, 2 * 1024 * 1024),
        name="pick",
    )(object_slices, after)


def sum_by_offset(received, after, classes):
    positions, _, width = received.shape
    columns = width - LANES

    def kernel(received, _, first, others):
        flags = [received[place, :, columns:].astype(F32) for place in range(positions)]
        for block in range(columns // LANES):
            lanes = slice(block * LANES, (block + 1) * LANES)
            values = [received[place, :, lanes].astype(F32) for place in range(positions)]
            for step in range(classes):
                picked = [
                    jnp.where(flag == float(step * STRIDE), value, 0.0)
                    for flag, value in zip(flags, values)
                ]
                while len(picked) > 1:
                    picked = [sum(picked[k + 1 : k + 2], picked[k]) for k in range(0, len(picked), 2)]
                if step == 0:
                    first[:, lanes] = picked[0].astype(BF16)
                else:
                    others[step - 1, :, lanes] = picked[0].astype(BF16)

    return pl.pallas_call(
        kernel,
        out_shape=(
            jax.ShapeDtypeStruct((16, columns), BF16),
            jax.ShapeDtypeStruct((classes - 1, 16, columns), BF16),
        ),
        in_specs=[whole(), whole(pl.ANY)],
        out_specs=(whole(), whole()),
        compiler_params=pltpu.CompilerParams(vmem_limit_bytes=VMEM_LIMIT),
        cost_estimate=cost(1, 1),
        name="sum_by_offset",
    )(received, after)


def object_of(own, layer, block):
    value = own[layer, :, block * LANES : (block + 1) * LANES].astype(F32)
    real, imag = value[:GROUP], value[GROUP:]
    return jnp.concatenate([real, real], axis=0), jnp.concatenate([imag, imag], axis=0)


def windows_of(padded, height, band):
    return jnp.concatenate([padded[pl.ds(step * 16, height), :] for step in range(band)], axis=1)


def forward(own_rows, probe_wave, propagator, classes):
    layers = own_rows.shape[0]
    columns = own_rows.shape[2]
    window_rows = probe_wave.shape[1]
    band = propagator.shape[1]
    blocks = columns // LANES
    centre = band // 2
    halves = classes // 2
    height = blocks * 16

    def kernel(own, probe, prop, waves, weights, padded_one, padded_two):
        padded = (padded_one, padded_two)
        scan = lax.axis_index("scan")
        odd = scan % 2 == 1
        for step in range(band):
            real, imag = prop[0, step], prop[1, step]
            top = step * 2 * LANES
            weights[top : top + LANES, :LANES] = real
            weights[top : top + LANES, LANES:] = imag
            weights[top + LANES : top + 2 * LANES, :LANES] = -imag
            weights[top + LANES : top + 2 * LANES, LANES:] = real
        for half in range(halves):
            padded[half][: centre * 16, :] = jnp.zeros((centre * 16, 2 * LANES), BF16)
            padded[half][(centre + blocks) * 16 :, :] = jnp.zeros(
                ((band - 1 - centre) * 16, 2 * LANES), BF16
            )
            for part in range(2):
                found = []
                for step in (2 * half, 2 * half + 1):
                    place = (scan - 2 * step + window_rows) % (window_rows // GROUP)
                    start = pl.multiple_of((place // 2) * 16, 16)
                    found.append(half_of(probe[part, pl.ds(start, 16), :].astype(F32), odd))
                found = jnp.concatenate(found, axis=0).astype(BF16)
                for block in range(blocks):
                    waves[0, half, block * 16 : (block + 1) * 16, part * LANES : (part + 1) * LANES] = (
                        found[:, block * LANES : (block + 1) * LANES]
                    )

        def transmit(layer, half):
            for block in range(blocks):
                at = slice(block * 16, (block + 1) * 16)
                wave_real = waves[layer, half, at, :LANES].astype(F32)
                wave_imag = waves[layer, half, at, LANES:].astype(F32)
                obj_real, obj_imag = object_of(own, layer, block)
                at = slice((block + centre) * 16, (block + centre + 1) * 16)
                padded[half][at, :LANES] = (obj_real * wave_real - obj_imag * wave_imag).astype(BF16)
                padded[half][at, LANES:] = (obj_real * wave_imag + obj_imag * wave_real).astype(BF16)

        def propagate(layer, half):
            field = jnp.dot(
                windows_of(padded[half], height, band), weights[...], preferred_element_type=F32
            )
            waves[layer + 1, half] = field.astype(BF16)

        transmit(0, 0)

        def layer_step(layer, carry):
            propagate(layer, 0)
            transmit(layer, 1)
            propagate(layer, 1)
            transmit(layer + 1, 0)
            return carry

        for layer in range(layers - 1):
            layer_step(layer, 0)

    flops = (layers - 1) * 4 * height * band * 4 * LANES * LANES
    padded = pltpu.VMEM(((blocks + band - 1) * 16, 2 * LANES), BF16)
    return pl.pallas_call(
        kernel,
        out_shape=jax.ShapeDtypeStruct((layers, halves, height, 2 * LANES), BF16),
        in_specs=[whole()] * 3,
        out_specs=whole(),
        scratch_shapes=[pltpu.VMEM((band * 2 * LANES, 2 * LANES), BF16), padded, padded],
        compiler_params=pltpu.CompilerParams(vmem_limit_bytes=VMEM_LIMIT),
        cost_estimate=cost(flops, 4 * 1024 * 1024),
        name="forward",
    )(own_rows, probe_wave, propagator)


def adjoint_weights(propagator, after):
    band = propagator.shape[1]

    def kernel(prop, _, weights):
        for step in range(band):
            real, imag = prop[0, step].T, prop[1, step].T
            top = (band - 1 - step) * 2 * LANES
            weights[top : top + LANES, :LANES] = real
            weights[top : top + LANES, LANES:] = -imag
            weights[top + LANES : top + 2 * LANES, :LANES] = imag
            weights[top + LANES : top + 2 * LANES, LANES:] = real

    return pl.pallas_call(
        kernel,
        out_shape=jax.ShapeDtypeStruct((band * 2 * LANES, 2 * LANES), BF16),
        in_specs=[whole(), whole(pl.ANY)],
        out_specs=whole(),
        compiler_params=pltpu.CompilerParams(vmem_limit_bytes=VMEM_LIMIT),
        cost_estimate=cost(0, 2 * 1024 * 1024),
        name="adjoint_weights",
    )(propagator, after)


def backward(first, others, incoming, waves, own_rows, weights, classes):
    layers = own_rows.shape[0]
    columns = own_rows.shape[2]
    blocks = columns // LANES
    band = weights.shape[0] // (2 * LANES)
    lead = band - 1 - band // 2
    halves = classes // 2
    height = blocks * 16

    def kernel(first, others, incoming, waves, own, weights, out, padded_one, padded_two, fields, terms):
        padded = (padded_one, padded_two)
        scan = lax.axis_index("scan")
        is_own = [scan >= 2 * step for step in range(classes)]
        for half in range(halves):
            padded[half][: lead * 16, :] = jnp.zeros((lead * 16, 2 * LANES), BF16)
            padded[half][(lead + blocks) * 16 :, :] = jnp.zeros(
                ((band - 1 - lead) * 16, 2 * LANES), BF16
            )
        for block in range(blocks):
            lanes = slice(block * LANES, (block + 1) * LANES)
            sums = [first[:, lanes].astype(F32)]
            for step in range(classes - 1):
                mine, other = others[step, :, lanes], incoming[step, :, lanes]
                sums.append(jnp.where(is_own[step + 1], mine, other).astype(F32))
            at = slice((block + lead) * 16, (block + lead + 1) * 16)
            for half in range(halves):
                pair = sums[2 * half : 2 * half + 2]
                padded[half][at, :LANES] = jnp.concatenate([s[:GROUP] for s in pair], axis=0).astype(BF16)
                padded[half][at, LANES:] = jnp.concatenate([s[GROUP:] for s in pair], axis=0).astype(BF16)

        def propagate(half):
            return jnp.dot(
                windows_of(padded[half], height, band), weights[...], preferred_element_type=F32
            )

        def meet(layer, half, field):
            for block in range(blocks):
                at = slice(block * 16, (block + 1) * 16)
                lanes = slice(block * LANES, (block + 1) * LANES)
                real, imag = field[at, :LANES], field[at, LANES:]
                wave_real = waves[layer, half, at, :LANES].astype(F32)
                wave_imag = waves[layer, half, at, LANES:].astype(F32)
                both = (
                    real * wave_real + imag * wave_imag,
                    imag * wave_real - real * wave_imag,
                )
                total = jnp.concatenate([term[:GROUP] + term[GROUP:] for term in both], axis=0)
                if half == 0:
                    terms[:, lanes] = total
                else:
                    slope = terms[:, lanes] + total
                    image = own[layer, :, lanes].astype(F32)
                    out[layer, :, lanes] = (image - STEP_SIZE * slope).astype(BF16)
                obj_real, obj_imag = object_of(own, layer, block)
                at = slice((block + lead) * 16, (block + lead + 1) * 16)
                padded[half][at, :LANES] = (real * obj_real + imag * obj_imag).astype(BF16)
                padded[half][at, LANES:] = (imag * obj_real - real * obj_imag).astype(BF16)

        fields[...] = propagate(0)

        def layer_step(index, carry):
            layer = layers - 1 - index
            second = propagate(1)
            meet(layer, 0, fields)
            fields[...] = propagate(0)
            meet(layer, 1, second)
            return carry

        for index in range(layers):
            layer_step(index, 0)

    flops = layers * 4 * height * band * 4 * LANES * LANES
    padded = pltpu.VMEM(((blocks + band - 1) * 16, 2 * LANES), BF16)
    return pl.pallas_call(
        kernel,
        out_shape=jax.ShapeDtypeStruct((layers, 2 * GROUP, columns), BF16),
        in_specs=[whole()] * 6,
        out_specs=whole(),
        scratch_shapes=[
            padded,
            padded,
            pltpu.VMEM((height, 2 * LANES), F32),
            pltpu.VMEM((2 * GROUP, columns), F32),
        ],
        compiler_params=pltpu.CompilerParams(vmem_limit_bytes=VMEM_LIMIT),
        cost_estimate=cost(flops, 4 * 1024 * 1024),
        name="backward",
    )(first, others, incoming, waves, own_rows, weights)


def iterate(plain, target, one, two, primal, part, span, last_rows):
    blocks = plain.shape[1]
    scale = DUAL_STEP / TV_WEIGHT
    lane = lax.broadcasted_iota(jnp.int32, (GROUP, LANES), 1)
    row = lax.broadcasted_iota(jnp.int32, (GROUP, LANES), 0)
    left_edge, right_edge = lane == 0, lane == LANES - 1
    zero = jnp.zeros((GROUP, LANES), F32)

    def at(ref, step):
        return [ref[part, b, step] for b in range(blocks)]

    def primal_of(duals, step, previous):
        dual, cols, base = at(duals[0], step), at(duals[1], step), at(target, step)
        turned = [pltpu.roll(v, 1, 1) for v in cols]
        result = []
        for b in range(blocks):
            moved = jnp.where(left_edge, turned[b - 1] if b else zero, turned[b])
            diverged = (dual[b] - previous[b]) + (cols[b] - moved)
            result.append(base[b] + (scale * TV_WEIGHT) * diverged)
        return result, dual

    def before_first(duals):
        return [jnp.where(row == 0, 0.0, pltpu.roll(v, 1, 0)) for v in at(duals[0], span - 1)]

    def ascend(duals, results, value, after, step):
        turned = [pltpu.roll(v, LANES - 1, 1) for v in value]
        dual, cols = (at(ref, step) for ref in duals) if duals else (None, None)
        for b in range(blocks):
            below = after[b]
            if step in last_rows:
                below = jnp.where(last_rows[step], value[b], below)
            right = turned[b + 1] if b + 1 < blocks else value[b]
            right = jnp.where(right_edge, right, turned[b])
            new_rows, new_cols = below - value[b], right - value[b]
            if duals:
                new_rows, new_cols = dual[b] + new_rows, cols[b] + new_cols
            shrink = jnp.minimum(1.0, lax.rsqrt(new_rows * new_rows + new_cols * new_cols))
            results[0][part, b, step] = new_rows * shrink
            results[1][part, b, step] = new_cols * shrink

    def sweep(duals, results):
        previous = before_first(duals)
        for step in range(span):
            value, previous = primal_of(duals, step, previous)
            for b in range(blocks):
                primal[part, b, step] = value[b]
                if step == 0:
                    primal[part, b, span] = pltpu.roll(value[b], GROUP - 1, 0)
        for step in range(span):
            ascend(duals, results, at(primal, step), at(primal, step + 1), step)

    values = [[plain[part, b, pl.ds(step, GROUP, stride=span), :] for b in range(blocks)] for step in range(2)]
    wrapped = [pltpu.roll(v, GROUP - 1, 0) for v in values[0]]
    for step in range(span):
        value, after = values
        for b in range(blocks):
            target[part, b, step] = value[b]
        ascend(None, one, value, after, step)
        if step + 2 < span:
            following = [plain[part, b, pl.ds(step + 2, GROUP, stride=span), :] for b in range(blocks)]
        else:
            following = wrapped
        values = [after, following]

    def twice(_, carry):
        sweep(one, two)
        sweep(two, one)
        return carry

    for _ in range((TV_ITERS - 1) // 2):
        twice(0, 0)
    last = one
    if TV_ITERS % 2 == 0:
        sweep(one, two)
        last = two
    previous = before_first(last)
    for step in range(span):
        result, previous = primal_of(last, step, previous)
        for b in range(blocks):
            plain[part, b, pl.ds(step, GROUP, stride=span), :] = result[b]


def denoise_scratch(span, blocks):
    buffer = pltpu.VMEM((2, blocks, span, GROUP, LANES), F32)
    return [
        pltpu.VMEM((2, blocks, span * GROUP, LANES), F32),
        buffer,
        buffer,
        buffer,
        buffer,
        buffer,
        pltpu.VMEM((2, blocks, span + 1, GROUP, LANES), F32),
    ]


def denoise(target_rows, from_even, from_odd):
    groups, _, columns = target_rows.shape
    rows = groups * GROUP
    span, blocks = groups + 2, columns // LANES
    tiles = lax.axis_size("tile")
    scale = DUAL_STEP / TV_WEIGHT
    above_at = divmod(GROUP - 1, span)
    last_at = divmod(GROUP + rows - 1, span)

    def kernel(
        own, even, odd, out, plain, target, rows_one, cols_one, rows_two, cols_two, primal, result, sems
    ):
        tile = lax.axis_index("tile")
        is_odd = tile % 2 == 1
        row = lax.broadcasted_iota(jnp.int32, (GROUP, LANES), 0)
        last_rows = {
            above_at[1]: (row == above_at[0]) & (tile == 0),
            last_at[1]: (row == last_at[0]) & (tile == tiles - 1),
        }
        values = [jnp.where(is_odd, even[0], odd[0])]
        values += [own[group] for group in range(groups)]
        values += [jnp.where(is_odd, odd[1], even[1])]
        for group, value in enumerate(values):
            value = scale * value.astype(F32)
            at = slice(group * GROUP, (group + 1) * GROUP)
            for b in range(blocks):
                lanes = slice(b * LANES, (b + 1) * LANES)
                plain[0, b, at] = value[:GROUP, lanes]
                plain[1, b, at] = value[GROUP:, lanes]
        copies = []
        for part in range(2):
            iterate(
                plain, target, (rows_one, cols_one), (rows_two, cols_two), primal, part, span, last_rows
            )
            for b in range(blocks):
                result[part, :, b * LANES : (b + 1) * LANES] = plain[part, b, GROUP : GROUP + rows] * (
                    1.0 / scale
                )
            copies.append(pltpu.make_async_copy(result.at[part], out.at[part, 0], sems.at[part]))
            copies[-1].start()
        for copy in copies:
            copy.wait()

    return pl.pallas_call(
        kernel,
        out_shape=jax.ShapeDtypeStruct((2, 1, rows, columns), F32),
        in_specs=[whole()] * 3,
        out_specs=whole(pltpu.HBM),
        scratch_shapes=denoise_scratch(span, blocks)
        + [pltpu.VMEM((2, rows, columns), F32), pltpu.SemaphoreType.DMA((2,))],
        compiler_params=pltpu.CompilerParams(vmem_limit_bytes=VMEM_LIMIT),
        cost_estimate=cost(0, 4 * 1024 * 1024),
        name="denoise",
    )(target_rows, from_even, from_odd)


def per_device(object_slices, probe_wave, propagator, offsets, adjoint):
    classes = probe_wave.shape[1] // STRIDE
    send = spread(offsets, adjoint)
    received = lax.all_to_all(send, "scan", 0, 0, tiled=True)
    own_rows = pick(object_slices, send)
    waves = forward(own_rows, probe_wave, propagator, classes)
    first, others = sum_by_offset(received, waves, classes)
    incoming = passed_along(others, "tile", 1)
    weights = adjoint_weights(propagator, others)
    chunks = backward(first, others, incoming, waves, own_rows, weights, classes)
    target_rows = lax.all_to_all(chunks, "scan", 0, 0, tiled=True)
    outward = jnp.concatenate([target_rows[-1:], target_rows[:1]], axis=0)
    return denoise(target_rows, swapped(outward, 0), swapped(outward, 1))


def solution(mesh):
    in_specs = (
        P(None, None, "tile", None),
        P(),
        P(),
        P("tile", "scan"),
        P(None, "tile", "scan", None, None),
    )
    out_specs = P(None, "scan", "tile", None)
    return jax.shard_map(
        per_device, mesh=mesh, in_specs=in_specs, out_specs=out_specs, check_vma=False
    )
```

```python
import jax
import jax.numpy as jnp
from jax import lax
from jax.experimental import pallas as pl
from jax.experimental.pallas import tpu as pltpu
from jax.sharding import PartitionSpec as P

STRIDE = 16
TV_ITERS = 6
STEP_SIZE = 0.5
TV_WEIGHT = 1.0
DUAL_STEP = 0.125

F32 = jnp.float32
BF16 = jnp.bfloat16
LANES = 128
GROUP = 8
VMEM_LIMIT = 32 * 1024 * 1024
PICK_LIMIT = 52 * 1024 * 1024


def swapped(value):
    pairs = [(even, even + 1) for even in range(0, lax.axis_size("tile"), 2)]
    return lax.ppermute(value, "tile", pairs + [(odd, even) for even, odd in pairs])


def whole(memory=pltpu.VMEM):
    return pl.BlockSpec(memory_space=memory)


def cost(flops, bytes_accessed):
    return pl.CostEstimate(flops=flops, bytes_accessed=bytes_accessed, transcendentals=0)


def half_of(block, odd):
    return jnp.where(odd, block[GROUP:], block[:GROUP])


def spread(offsets, adjoint):
    rows, columns = adjoint.shape[3:]
    groups = rows // GROUP
    pairs = groups // 2

    def kernel(field, offset_ref, send):
        offset = jnp.broadcast_to(offset_ref[...], (16, LANES))
        flag = offset.astype(F32).astype(BF16)
        steps = [
            jnp.broadcast_to(offset_ref[...], (16, columns)) == step * STRIDE for step in range(pairs)
        ]
        groups_of = [
            [field[part, 0, 0, pair * 16 : (pair + 1) * 16, :].astype(F32) for pair in range(pairs)]
            for part in range(2)
        ]
        for pair in range(pairs):
            turned = []
            for part in range(2):
                value = groups_of[part][pair]
                for step in range(1, pairs):
                    value = jnp.where(steps[step], groups_of[part][(pair - step) % pairs], value)
                turned.append(value)
            for half in range(2):
                part = slice(half * GROUP, (half + 1) * GROUP)
                value = jnp.concatenate([value[part] for value in turned], axis=0).astype(BF16)
                for copy in range(2):
                    send[copy * groups + 2 * pair + half, :, :columns] = value
                    send[copy * groups + 2 * pair + half, :, columns:] = flag

    return pl.pallas_call(
        kernel,
        out_shape=jax.ShapeDtypeStruct((2 * groups, 16, columns + LANES), BF16),
        in_specs=[whole(), whole()],
        out_specs=whole(),
        compiler_params=pltpu.CompilerParams(vmem_limit_bytes=VMEM_LIMIT),
        cost_estimate=cost(0, 512 * 1024),
        name="spread",
    )(adjoint, offsets)


def pick(object_slices, after):
    layers, _, columns = object_slices.shape[1:]

    def kernel(object_hbm, _, own_rows, block, sem):
        scan = lax.axis_index("scan")
        start = pl.multiple_of((scan // 2) * 16, 16)
        copy = pltpu.make_async_copy(object_hbm.at[:, :, pl.ds(start, 16), :], block, sem)
        copy.start()
        copy.wait()
        odd = scan % 2 == 1
        for layer in range(layers):
            own_rows[layer] = jnp.concatenate(
                [half_of(block[part, layer].astype(F32), odd) for part in range(2)], axis=0
            ).astype(BF16)

    return pl.pallas_call(
        kernel,
        out_shape=jax.ShapeDtypeStruct((layers, 16, columns), BF16),
        in_specs=[whole(pltpu.HBM), whole(pl.ANY)],
        out_specs=whole(),
        scratch_shapes=[pltpu.VMEM((2, layers, 16, columns), BF16), pltpu.SemaphoreType.DMA],
        compiler_params=pltpu.CompilerParams(vmem_limit_bytes=PICK_LIMIT),
        cost_estimate=cost(0, 2 * 1024 * 1024),
        name="pick",
    )(object_slices, after)


def sum_by_offset(received, after, classes):
    positions, _, width = received.shape
    positions = positions // 2
    columns = width - LANES

    def kernel(received, _, first, others, beside):
        is_even = 1 - lax.axis_index("tile") % 2

        def sums_of(start, steps):
            flags = [received[start + k, :, columns:].astype(F32) for k in range(positions)]
            for block in range(columns // LANES):
                lanes = slice(block * LANES, (block + 1) * LANES)
                values = [received[start + k, :, lanes].astype(F32) for k in range(positions)]
                for step in steps:
                    picked = [
                        jnp.where(flag == float(step * STRIDE), value, 0.0)
                        for flag, value in zip(flags, values)
                    ]
                    while len(picked) > 1:
                        picked = [sum(picked[k + 1 : k + 2], picked[k]) for k in range(0, len(picked), 2)]
                    yield step, lanes, picked[0].astype(BF16)

        for step, lanes, value in sums_of(is_even * positions, range(classes)):
            if step == 0:
                first[:, lanes] = value
            else:
                others[step - 1, :, lanes] = value
        for step, lanes, value in sums_of((1 - is_even) * positions, range(1, classes)):
            beside[step - 1, :, lanes] = value

    several = jax.ShapeDtypeStruct((classes - 1, 16, columns), BF16)
    return pl.pallas_call(
        kernel,
        out_shape=(jax.ShapeDtypeStruct((16, columns), BF16), several, several),
        in_specs=[whole(), whole(pl.ANY)],
        out_specs=(whole(), whole(), whole()),
        compiler_params=pltpu.CompilerParams(vmem_limit_bytes=VMEM_LIMIT),
        cost_estimate=cost(1, 1),
        name="sum_by_offset",
    )(received, after)


def object_of(own, layer, block):
    value = own[layer, :, block * LANES : (block + 1) * LANES].astype(F32)
    real, imag = value[:GROUP], value[GROUP:]
    return jnp.concatenate([real, real], axis=0), jnp.concatenate([imag, imag], axis=0)


def windows_of(padded, height, band):
    return jnp.concatenate([padded[pl.ds(step * 16, height), :] for step in range(band)], axis=1)


def forward(own_rows, probe_wave, propagator, classes):
    layers = own_rows.shape[0]
    columns = own_rows.shape[2]
    window_rows = probe_wave.shape[1]
    band = propagator.shape[1]
    blocks = columns // LANES
    centre = band // 2
    halves = classes // 2
    height = blocks * 16

    def kernel(own, probe, prop, waves, weights, padded_one, padded_two):
        padded = (padded_one, padded_two)
        scan = lax.axis_index("scan")
        odd = scan % 2 == 1
        for step in range(band):
            real, imag = prop[0, step], prop[1, step]
            top = step * 2 * LANES
            weights[top : top + LANES, :LANES] = real
            weights[top : top + LANES, LANES:] = imag
            weights[top + LANES : top + 2 * LANES, :LANES] = -imag
            weights[top + LANES : top + 2 * LANES, LANES:] = real
        for half in range(halves):
            padded[half][: centre * 16, :] = jnp.zeros((centre * 16, 2 * LANES), BF16)
            padded[half][(centre + blocks) * 16 :, :] = jnp.zeros(
                ((band - 1 - centre) * 16, 2 * LANES), BF16
            )
            for part in range(2):
                found = []
                for step in (2 * half, 2 * half + 1):
                    place = (scan - 2 * step + window_rows) % (window_rows // GROUP)
                    start = pl.multiple_of((place // 2) * 16, 16)
                    found.append(half_of(probe[part, pl.ds(start, 16), :].astype(F32), odd))
                found = jnp.concatenate(found, axis=0).astype(BF16)
                for block in range(blocks):
                    waves[0, half, block * 16 : (block + 1) * 16, part * LANES : (part + 1) * LANES] = (
                        found[:, block * LANES : (block + 1) * LANES]
                    )

        def transmit(layer, half):
            for block in range(blocks):
                at = slice(block * 16, (block + 1) * 16)
                wave_real = waves[layer, half, at, :LANES].astype(F32)
                wave_imag = waves[layer, half, at, LANES:].astype(F32)
                obj_real, obj_imag = object_of(own, layer, block)
                at = slice((block + centre) * 16, (block + centre + 1) * 16)
                padded[half][at, :LANES] = (obj_real * wave_real - obj_imag * wave_imag).astype(BF16)
                padded[half][at, LANES:] = (obj_real * wave_imag + obj_imag * wave_real).astype(BF16)

        def propagate(layer, half):
            field = jnp.dot(
                windows_of(padded[half], height, band), weights[...], preferred_element_type=F32
            )
            waves[layer + 1, half] = field.astype(BF16)

        transmit(0, 0)

        def layer_step(layer, carry):
            propagate(layer, 0)
            transmit(layer, 1)
            propagate(layer, 1)
            if layer + 1 < layers - 1:
                transmit(layer + 1, 0)
            return carry

        for layer in range(layers - 1):
            layer_step(layer, 0)

    flops = (layers - 1) * 4 * height * band * 4 * LANES * LANES
    padded = pltpu.VMEM(((blocks + band - 1) * 16, 2 * LANES), BF16)
    return pl.pallas_call(
        kernel,
        out_shape=jax.ShapeDtypeStruct((layers, halves, height, 2 * LANES), BF16),
        in_specs=[whole()] * 3,
        out_specs=whole(),
        scratch_shapes=[pltpu.VMEM((band * 2 * LANES, 2 * LANES), BF16), padded, padded],
        compiler_params=pltpu.CompilerParams(vmem_limit_bytes=VMEM_LIMIT),
        cost_estimate=cost(flops, 4 * 1024 * 1024),
        name="forward",
    )(own_rows, probe_wave, propagator)


def adjoint_weights(propagator, after):
    band = propagator.shape[1]

    def kernel(prop, _, weights):
        for step in range(band):
            real, imag = prop[0, step].T, prop[1, step].T
            top = (band - 1 - step) * 2 * LANES
            weights[top : top + LANES, :LANES] = real
            weights[top : top + LANES, LANES:] = -imag
            weights[top + LANES : top + 2 * LANES, :LANES] = imag
            weights[top + LANES : top + 2 * LANES, LANES:] = real

    return pl.pallas_call(
        kernel,
        out_shape=jax.ShapeDtypeStruct((band * 2 * LANES, 2 * LANES), BF16),
        in_specs=[whole(), whole(pl.ANY)],
        out_specs=whole(),
        compiler_params=pltpu.CompilerParams(vmem_limit_bytes=VMEM_LIMIT),
        cost_estimate=cost(0, 2 * 1024 * 1024),
        name="adjoint_weights",
    )(propagator, after)


def backward(first, others, beside, from_chip, waves, own_rows, weights, classes):
    layers = own_rows.shape[0]
    columns = own_rows.shape[2]
    blocks = columns // LANES
    band = weights.shape[0] // (2 * LANES)
    lead = band - 1 - band // 2
    halves = classes // 2
    height = blocks * 16

    def kernel(first, others, beside, from_chip, waves, own, weights, out, padded_one, padded_two, fields, terms):
        padded = (padded_one, padded_two)
        scan = lax.axis_index("scan")
        is_odd = lax.axis_index("tile") % 2 == 1
        is_own = [scan >= 2 * step for step in range(classes)]
        for half in range(halves):
            padded[half][: lead * 16, :] = jnp.zeros((lead * 16, 2 * LANES), BF16)
            padded[half][(lead + blocks) * 16 :, :] = jnp.zeros(
                ((band - 1 - lead) * 16, 2 * LANES), BF16
            )
        for block in range(blocks):
            lanes = slice(block * LANES, (block + 1) * LANES)
            sums = [first[:, lanes].astype(F32)]
            for step in range(classes - 1):
                mine = others[step, :, lanes]
                other = jnp.where(is_odd, from_chip[step, :, lanes], beside[step, :, lanes])
                sums.append(jnp.where(is_own[step + 1], mine, other).astype(F32))
            at = slice((block + lead) * 16, (block + lead + 1) * 16)
            for half in range(halves):
                pair = sums[2 * half : 2 * half + 2]
                padded[half][at, :LANES] = jnp.concatenate([s[:GROUP] for s in pair], axis=0).astype(BF16)
                padded[half][at, LANES:] = jnp.concatenate([s[GROUP:] for s in pair], axis=0).astype(BF16)

        def propagate(half):
            return jnp.dot(
                windows_of(padded[half], height, band), weights[...], preferred_element_type=F32
            )

        def meet(layer, half, field):
            for block in range(blocks):
                at = slice(block * 16, (block + 1) * 16)
                lanes = slice(block * LANES, (block + 1) * LANES)
                real, imag = field[at, :LANES], field[at, LANES:]
                wave_real = waves[layer, half, at, :LANES].astype(F32)
                wave_imag = waves[layer, half, at, LANES:].astype(F32)
                both = (
                    real * wave_real + imag * wave_imag,
                    imag * wave_real - real * wave_imag,
                )
                total = jnp.concatenate([term[:GROUP] + term[GROUP:] for term in both], axis=0)
                if half == 0:
                    terms[:, lanes] = total
                else:
                    slope = terms[:, lanes] + total
                    image = own[layer, :, lanes].astype(F32)
                    value = (image - STEP_SIZE * slope).astype(BF16)
                    out[layer, :, lanes] = value
                    out[layers + layer, :, lanes] = value
                if layer == 0:
                    continue
                obj_real, obj_imag = object_of(own, layer, block)
                at = slice((block + lead) * 16, (block + lead + 1) * 16)
                padded[half][at, :LANES] = (real * obj_real + imag * obj_imag).astype(BF16)
                padded[half][at, LANES:] = (imag * obj_real - real * obj_imag).astype(BF16)

        fields[...] = propagate(0)

        def layer_step(index, carry):
            layer = layers - 1 - index
            second = propagate(1)
            meet(layer, 0, fields)
            if layer:
                fields[...] = propagate(0)
            meet(layer, 1, second)
            return carry

        for index in range(layers):
            layer_step(index, 0)

    flops = layers * 4 * height * band * 4 * LANES * LANES
    padded = pltpu.VMEM(((blocks + band - 1) * 16, 2 * LANES), BF16)
    return pl.pallas_call(
        kernel,
        out_shape=jax.ShapeDtypeStruct((2 * layers, 2 * GROUP, columns), BF16),
        in_specs=[whole()] * 7,
        out_specs=whole(),
        scratch_shapes=[
            padded,
            padded,
            pltpu.VMEM((height, 2 * LANES), F32),
            pltpu.VMEM((2 * GROUP, columns), F32),
        ],
        compiler_params=pltpu.CompilerParams(vmem_limit_bytes=VMEM_LIMIT),
        cost_estimate=cost(flops, 4 * 1024 * 1024),
        name="backward",
    )(first, others, beside, from_chip, waves, own_rows, weights)


def iterate(plain, target, one, two, primal, part, span, last_rows):
    blocks = plain.shape[1]
    scale = DUAL_STEP / TV_WEIGHT
    lane = lax.broadcasted_iota(jnp.int32, (GROUP, LANES), 1)
    row = lax.broadcasted_iota(jnp.int32, (GROUP, LANES), 0)
    left_edge, right_edge = lane == 0, lane == LANES - 1
    zero = jnp.zeros((GROUP, LANES), F32)

    def at(ref, step):
        return [ref[part, b, step] for b in range(blocks)]

    def primal_of(duals, step, previous):
        dual, cols, base = at(duals[0], step), at(duals[1], step), at(target, step)
        turned = [pltpu.roll(v, 1, 1) for v in cols]
        result = []
        for b in range(blocks):
            moved = jnp.where(left_edge, turned[b - 1] if b else zero, turned[b])
            diverged = (dual[b] - previous[b]) + (cols[b] - moved)
            result.append(base[b] + (scale * TV_WEIGHT) * diverged)
        return result, dual

    def before_first(duals):
        return [jnp.where(row == 0, 0.0, pltpu.roll(v, 1, 0)) for v in at(duals[0], span - 1)]

    def ascend(duals, results, value, after, step):
        turned = [pltpu.roll(v, LANES - 1, 1) for v in value]
        dual, cols = (at(ref, step) for ref in duals) if duals else (None, None)
        for b in range(blocks):
            below = after[b]
            if step in last_rows:
                below = jnp.where(last_rows[step], value[b], below)
            right = turned[b + 1] if b + 1 < blocks else value[b]
            right = jnp.where(right_edge, right, turned[b])
            new_rows, new_cols = below - value[b], right - value[b]
            if duals:
                new_rows, new_cols = dual[b] + new_rows, cols[b] + new_cols
            shrink = jnp.minimum(1.0, lax.rsqrt(new_rows * new_rows + new_cols * new_cols))
            results[0][part, b, step] = new_rows * shrink
            results[1][part, b, step] = new_cols * shrink

    def sweep(duals, results):
        previous = before_first(duals)
        for step in range(span):
            value, previous = primal_of(duals, step, previous)
            for b in range(blocks):
                primal[part, b, step] = value[b]
                if step == 0:
                    primal[part, b, span] = pltpu.roll(value[b], GROUP - 1, 0)
        for step in range(span):
            ascend(duals, results, at(primal, step), at(primal, step + 1), step)

    values = [[plain[part, b, pl.ds(step, GROUP, stride=span), :] for b in range(blocks)] for step in range(2)]
    wrapped = [pltpu.roll(v, GROUP - 1, 0) for v in values[0]]
    for step in range(span):
        value, after = values
        for b in range(blocks):
            target[part, b, step] = value[b]
        ascend(None, one, value, after, step)
        if step + 2 < span:
            following = [plain[part, b, pl.ds(step + 2, GROUP, stride=span), :] for b in range(blocks)]
        else:
            following = wrapped
        values = [after, following]

    def twice(_, carry):
        sweep(one, two)
        sweep(two, one)
        return carry

    for _ in range((TV_ITERS - 1) // 2):
        twice(0, 0)
    last = one
    if TV_ITERS % 2 == 0:
        sweep(one, two)
        last = two
    previous = before_first(last)
    for step in range(span):
        result, previous = primal_of(last, step, previous)
        for b in range(blocks):
            plain[part, b, pl.ds(step, GROUP, stride=span), :] = result[b]


def denoise_scratch(span, blocks):
    buffer = pltpu.VMEM((2, blocks, span, GROUP, LANES), F32)
    return [
        pltpu.VMEM((2, blocks, span * GROUP, LANES), F32),
        buffer,
        buffer,
        buffer,
        buffer,
        buffer,
        pltpu.VMEM((2, blocks, span + 1, GROUP, LANES), F32),
    ]


def denoise(target_rows, from_chip):
    groups, _, columns = target_rows.shape
    groups = groups // 2
    rows = groups * GROUP
    span, blocks = groups + 2, columns // LANES
    tiles = lax.axis_size("tile")
    scale = DUAL_STEP / TV_WEIGHT
    above_at = divmod(GROUP - 1, span)
    last_at = divmod(GROUP + rows - 1, span)

    def kernel(
        pieces, chip, out, plain, target, rows_one, cols_one, rows_two, cols_two, primal, result, sems
    ):
        tile = lax.axis_index("tile")
        is_odd = tile % 2 == 1
        row = lax.broadcasted_iota(jnp.int32, (GROUP, LANES), 0)
        last_rows = {
            above_at[1]: (row == above_at[0]) & (tile == 0),
            last_at[1]: (row == last_at[0]) & (tile == tiles - 1),
        }
        start = (1 - tile % 2) * groups
        values = [jnp.where(is_odd, chip[1], pieces[groups - 1])]
        values += [pieces[start + group] for group in range(groups)]
        values += [jnp.where(is_odd, pieces[groups], chip[0])]
        for group, value in enumerate(values):
            value = scale * value.astype(F32)
            at = slice(group * GROUP, (group + 1) * GROUP)
            for b in range(blocks):
                lanes = slice(b * LANES, (b + 1) * LANES)
                plain[0, b, at] = value[:GROUP, lanes]
                plain[1, b, at] = value[GROUP:, lanes]
        copies = []
        for part in range(2):
            iterate(
                plain, target, (rows_one, cols_one), (rows_two, cols_two), primal, part, span, last_rows
            )
            for b in range(blocks):
                result[part, :, b * LANES : (b + 1) * LANES] = plain[part, b, GROUP : GROUP + rows] * (
                    1.0 / scale
                )
            copies.append(pltpu.make_async_copy(result.at[part], out.at[part, 0], sems.at[part]))
            copies[-1].start()
        for copy in copies:
            copy.wait()

    return pl.pallas_call(
        kernel,
        out_shape=jax.ShapeDtypeStruct((2, 1, rows, columns), F32),
        in_specs=[whole()] * 2,
        out_specs=whole(pltpu.HBM),
        scratch_shapes=denoise_scratch(span, blocks)
        + [pltpu.VMEM((2, rows, columns), F32), pltpu.SemaphoreType.DMA((2,))],
        compiler_params=pltpu.CompilerParams(vmem_limit_bytes=VMEM_LIMIT),
        cost_estimate=cost(0, 4 * 1024 * 1024),
        name="denoise",
    )(target_rows, from_chip)


def exchanged(value, tiles, scans):
    groups = [
        [tile % tiles * scans + scan for tile in (odd, odd + 1) for scan in range(scans)]
        for odd in range(1, tiles, 2)
    ]
    return lax.all_to_all(value, ("tile", "scan"), 0, 0, tiled=True, axis_index_groups=groups)


def per_device(object_slices, probe_wave, propagator, offsets, adjoint):
    classes = probe_wave.shape[1] // STRIDE
    tiles, scans = lax.axis_size("tile"), lax.axis_size("scan")
    send = spread(offsets, adjoint)
    received = exchanged(send, tiles, scans)
    own_rows = pick(object_slices, send)
    waves = forward(own_rows, probe_wave, propagator, classes)
    first, others, beside = sum_by_offset(received, waves, classes)
    from_chip = swapped(others)
    weights = adjoint_weights(propagator, others)
    chunks = backward(first, others, beside, from_chip, waves, own_rows, weights, classes)
    target_rows = exchanged(chunks, tiles, scans)
    outward = jnp.concatenate([target_rows[:1], target_rows[-1:]], axis=0)
    return denoise(target_rows, swapped(outward))


def solution(mesh):
    in_specs = (
        P(None, None, "tile", None),
        P(),
        P(),
        P("tile", "scan"),
        P(None, "tile", "scan", None, None),
    )
    out_specs = P(None, "scan", "tile", None)
    return jax.shard_map(
        per_device, mesh=mesh, in_specs=in_specs, out_specs=out_specs, check_vma=False
    )
```

```python
import jax
import jax.numpy as jnp
from jax import lax
from jax.experimental import pallas as pl
from jax.experimental.pallas import tpu as pltpu
from jax.sharding import PartitionSpec as P

STRIDE = 16
TV_ITERS = 6
STEP_SIZE = 0.5
TV_WEIGHT = 1.0
DUAL_STEP = 0.125

F32 = jnp.float32
BF16 = jnp.bfloat16
LANES = 128
GROUP = 8
VMEM_LIMIT = 32 * 1024 * 1024
PICK_LIMIT = 52 * 1024 * 1024


def swapped(value):
    pairs = [(even, even + 1) for even in range(0, lax.axis_size("tile"), 2)]
    return lax.ppermute(value, "tile", pairs + [(odd, even) for even, odd in pairs])


def whole(memory=pltpu.VMEM):
    return pl.BlockSpec(memory_space=memory)


def cost(flops, bytes_accessed):
    return pl.CostEstimate(flops=flops, bytes_accessed=bytes_accessed, transcendentals=0)


def half_of(block, odd):
    return jnp.where(odd, block[GROUP:], block[:GROUP])


def spread(offsets, adjoint):
    rows, columns = adjoint.shape[3:]
    groups = rows // GROUP
    pairs = groups // 2

    def kernel(field, offset_ref, send):
        offset = offset_ref[0, 0]
        steps = offset // STRIDE
        flag = jnp.full((16, LANES), offset, jnp.int32).astype(F32).astype(BF16)
        for pair in range(pairs):
            source = pl.multiple_of(((pair - steps + pairs) % pairs) * 16, 16)
            turned = [field[part, 0, 0, pl.ds(source, 16), :].astype(F32) for part in range(2)]
            for half in range(2):
                part = slice(half * GROUP, (half + 1) * GROUP)
                value = jnp.concatenate([value[part] for value in turned], axis=0).astype(BF16)
                for copy in range(2):
                    send[2 * (2 * pair + half) + copy, :, :columns] = value
                    send[2 * (2 * pair + half) + copy, :, columns:] = flag

    return pl.pallas_call(
        kernel,
        out_shape=jax.ShapeDtypeStruct((2 * groups, 16, columns + LANES), BF16),
        in_specs=[whole(), whole(pltpu.SMEM)],
        out_specs=whole(),
        compiler_params=pltpu.CompilerParams(vmem_limit_bytes=VMEM_LIMIT),
        cost_estimate=cost(0, 512 * 1024),
        name="spread",
    )(adjoint, offsets)


def pick(object_slices, after):
    layers, _, columns = object_slices.shape[1:]

    def kernel(object_hbm, _, own_rows, block, sem):
        scan = lax.axis_index("scan")
        start = pl.multiple_of((scan // 2) * 16, 16)
        copy = pltpu.make_async_copy(object_hbm.at[:, :, pl.ds(start, 16), :], block, sem)
        copy.start()
        copy.wait()
        odd = scan % 2 == 1
        for layer in range(layers):
            own_rows[layer] = jnp.concatenate(
                [half_of(block[part, layer].astype(F32), odd) for part in range(2)], axis=0
            ).astype(BF16)

    return pl.pallas_call(
        kernel,
        out_shape=jax.ShapeDtypeStruct((layers, 16, columns), BF16),
        in_specs=[whole(pltpu.HBM), whole(pl.ANY)],
        out_specs=whole(),
        scratch_shapes=[pltpu.VMEM((2, layers, 16, columns), BF16), pltpu.SemaphoreType.DMA],
        compiler_params=pltpu.CompilerParams(vmem_limit_bytes=PICK_LIMIT),
        cost_estimate=cost(0, 2 * 1024 * 1024),
        name="pick",
    )(object_slices, after)


def sum_by_offset(received, after, classes, wanted, name):
    positions, _, width = received.shape
    positions = positions // 2
    columns = width - LANES

    def kernel(received, _, out):
        is_even = 1 - lax.axis_index("tile") % 2
        for other in sorted({tile for tile, _ in wanted}):
            start = (1 - is_even) if other else is_even
            flags = [received[2 * k + start, :, columns:].astype(F32) for k in range(positions)]
            for block in range(columns // LANES):
                lanes = slice(block * LANES, (block + 1) * LANES)
                values = [received[2 * k + start, :, lanes].astype(F32) for k in range(positions)]
                for at, (tile, step) in enumerate(wanted):
                    if tile != other:
                        continue
                    picked = [
                        jnp.where(flag == float(step * STRIDE), value, 0.0)
                        for flag, value in zip(flags, values)
                    ]
                    while len(picked) > 1:
                        picked = [sum(picked[k + 1 : k + 2], picked[k]) for k in range(0, len(picked), 2)]
                    out[at, :, lanes] = picked[0].astype(BF16)

    return pl.pallas_call(
        kernel,
        out_shape=jax.ShapeDtypeStruct((len(wanted), 16, columns), BF16),
        in_specs=[whole(), whole(pl.ANY)],
        out_specs=whole(),
        compiler_params=pltpu.CompilerParams(vmem_limit_bytes=VMEM_LIMIT),
        cost_estimate=cost(0, 1024 * 1024),
        name=name,
    )(received, after)


def object_of(own, layer, block):
    value = own[layer, :, block * LANES : (block + 1) * LANES].astype(F32)
    real, imag = value[:GROUP], value[GROUP:]
    return jnp.concatenate([real, real], axis=0), jnp.concatenate([imag, imag], axis=0)


def windows_of(padded, height, band):
    return jnp.concatenate([padded[pl.ds(step * 16, height), :] for step in range(band)], axis=1)


def forward(own_rows, probe_wave, propagator, classes):
    layers = own_rows.shape[0]
    columns = own_rows.shape[2]
    window_rows = probe_wave.shape[1]
    band = propagator.shape[1]
    blocks = columns // LANES
    centre = band // 2
    halves = classes // 2
    height = blocks * 16

    def kernel(own, probe, prop, waves, weights, padded_one, padded_two):
        padded = (padded_one, padded_two)
        scan = lax.axis_index("scan")
        odd = scan % 2 == 1
        for step in range(band):
            real, imag = prop[0, step], prop[1, step]
            top = step * 2 * LANES
            weights[top : top + LANES, :LANES] = real
            weights[top : top + LANES, LANES:] = imag
            weights[top + LANES : top + 2 * LANES, :LANES] = -imag
            weights[top + LANES : top + 2 * LANES, LANES:] = real
        for half in range(halves):
            padded[half][: centre * 16, :] = jnp.zeros((centre * 16, 2 * LANES), BF16)
            padded[half][(centre + blocks) * 16 :, :] = jnp.zeros(
                ((band - 1 - centre) * 16, 2 * LANES), BF16
            )
            for part in range(2):
                found = []
                for step in (2 * half, 2 * half + 1):
                    place = (scan - 2 * step + window_rows) % (window_rows // GROUP)
                    start = pl.multiple_of((place // 2) * 16, 16)
                    found.append(half_of(probe[part, pl.ds(start, 16), :].astype(F32), odd))
                found = jnp.concatenate(found, axis=0).astype(BF16)
                for block in range(blocks):
                    waves[0, half, block * 16 : (block + 1) * 16, part * LANES : (part + 1) * LANES] = (
                        found[:, block * LANES : (block + 1) * LANES]
                    )

        def transmit(layer, half):
            for block in range(blocks):
                at = slice(block * 16, (block + 1) * 16)
                wave_real = waves[layer, half, at, :LANES].astype(F32)
                wave_imag = waves[layer, half, at, LANES:].astype(F32)
                obj_real, obj_imag = object_of(own, layer, block)
                at = slice((block + centre) * 16, (block + centre + 1) * 16)
                padded[half][at, :LANES] = (obj_real * wave_real - obj_imag * wave_imag).astype(BF16)
                padded[half][at, LANES:] = (obj_real * wave_imag + obj_imag * wave_real).astype(BF16)

        def propagate(layer, half):
            field = jnp.dot(
                windows_of(padded[half], height, band), weights[...], preferred_element_type=F32
            )
            waves[layer + 1, half] = field.astype(BF16)

        transmit(0, 0)

        def layer_step(layer, carry):
            propagate(layer, 0)
            transmit(layer, 1)
            propagate(layer, 1)
            if layer + 1 < layers - 1:
                transmit(layer + 1, 0)
            return carry

        for layer in range(layers - 1):
            layer_step(layer, 0)

    flops = (layers - 1) * 4 * height * band * 4 * LANES * LANES
    padded = pltpu.VMEM(((blocks + band - 1) * 16, 2 * LANES), BF16)
    return pl.pallas_call(
        kernel,
        out_shape=jax.ShapeDtypeStruct((layers, halves, height, 2 * LANES), BF16),
        in_specs=[whole()] * 3,
        out_specs=whole(),
        scratch_shapes=[pltpu.VMEM((band * 2 * LANES, 2 * LANES), BF16), padded, padded],
        compiler_params=pltpu.CompilerParams(vmem_limit_bytes=VMEM_LIMIT),
        cost_estimate=cost(flops, 4 * 1024 * 1024),
        name="forward",
    )(own_rows, probe_wave, propagator)


def adjoint_weights(propagator, after):
    band = propagator.shape[1]

    def kernel(prop, _, weights):
        for step in range(band):
            real, imag = prop[0, step].T, prop[1, step].T
            top = (band - 1 - step) * 2 * LANES
            weights[top : top + LANES, :LANES] = real
            weights[top : top + LANES, LANES:] = -imag
            weights[top + LANES : top + 2 * LANES, :LANES] = imag
            weights[top + LANES : top + 2 * LANES, LANES:] = real

    return pl.pallas_call(
        kernel,
        out_shape=jax.ShapeDtypeStruct((band * 2 * LANES, 2 * LANES), BF16),
        in_specs=[whole(), whole(pl.ANY)],
        out_specs=whole(),
        compiler_params=pltpu.CompilerParams(vmem_limit_bytes=VMEM_LIMIT),
        cost_estimate=cost(0, 2 * 1024 * 1024),
        name="adjoint_weights",
    )(propagator, after)


def backward(rest, others, from_chip, waves, own_rows, weights, classes):
    layers = own_rows.shape[0]
    columns = own_rows.shape[2]
    blocks = columns // LANES
    band = weights.shape[0] // (2 * LANES)
    lead = band - 1 - band // 2
    halves = classes // 2
    height = blocks * 16

    def kernel(rest, others, from_chip, waves, own, weights, out, padded_one, padded_two, fields, terms):
        padded = (padded_one, padded_two)
        scan = lax.axis_index("scan")
        is_odd = lax.axis_index("tile") % 2 == 1
        is_own = [scan >= 2 * step for step in range(classes)]
        for half in range(halves):
            padded[half][: lead * 16, :] = jnp.zeros((lead * 16, 2 * LANES), BF16)
            padded[half][(lead + blocks) * 16 :, :] = jnp.zeros(
                ((band - 1 - lead) * 16, 2 * LANES), BF16
            )
        for block in range(blocks):
            lanes = slice(block * LANES, (block + 1) * LANES)
            sums = [rest[0, :, lanes].astype(F32)]
            for step in range(classes - 1):
                mine = others[step, :, lanes]
                other = jnp.where(is_odd, from_chip[step, :, lanes], rest[step + 1, :, lanes])
                sums.append(jnp.where(is_own[step + 1], mine, other).astype(F32))
            at = slice((block + lead) * 16, (block + lead + 1) * 16)
            for half in range(halves):
                pair = sums[2 * half : 2 * half + 2]
                padded[half][at, :LANES] = jnp.concatenate([s[:GROUP] for s in pair], axis=0).astype(BF16)
                padded[half][at, LANES:] = jnp.concatenate([s[GROUP:] for s in pair], axis=0).astype(BF16)

        def propagate(half):
            return jnp.dot(
                windows_of(padded[half], height, band), weights[...], preferred_element_type=F32
            )

        def meet(layer, half, field):
            for block in range(blocks):
                at = slice(block * 16, (block + 1) * 16)
                lanes = slice(block * LANES, (block + 1) * LANES)
                real, imag = field[at, :LANES], field[at, LANES:]
                wave_real = waves[layer, half, at, :LANES].astype(F32)
                wave_imag = waves[layer, half, at, LANES:].astype(F32)
                both = (
                    real * wave_real + imag * wave_imag,
                    imag * wave_real - real * wave_imag,
                )
                total = jnp.concatenate([term[:GROUP] + term[GROUP:] for term in both], axis=0)
                if half == 0:
                    terms[:, lanes] = total
                else:
                    slope = terms[:, lanes] + total
                    image = own[layer, :, lanes].astype(F32)
                    value = (image - STEP_SIZE * slope).astype(BF16)
                    out[2 * layer, :, lanes] = value
                    out[2 * layer + 1, :, lanes] = value
                if layer == 0:
                    continue
                obj_real, obj_imag = object_of(own, layer, block)
                at = slice((block + lead) * 16, (block + lead + 1) * 16)
                padded[half][at, :LANES] = (real * obj_real + imag * obj_imag).astype(BF16)
                padded[half][at, LANES:] = (imag * obj_real - real * obj_imag).astype(BF16)

        fields[...] = propagate(0)

        def layer_step(index, carry):
            layer = layers - 1 - index
            second = propagate(1)
            meet(layer, 0, fields)
            if layer:
                fields[...] = propagate(0)
            meet(layer, 1, second)
            return carry

        for index in range(layers):
            layer_step(index, 0)

    flops = layers * 4 * height * band * 4 * LANES * LANES
    padded = pltpu.VMEM(((blocks + band - 1) * 16, 2 * LANES), BF16)
    return pl.pallas_call(
        kernel,
        out_shape=jax.ShapeDtypeStruct((2 * layers, 2 * GROUP, columns), BF16),
        in_specs=[whole()] * 6,
        out_specs=whole(),
        scratch_shapes=[
            padded,
            padded,
            pltpu.VMEM((height, 2 * LANES), F32),
            pltpu.VMEM((2 * GROUP, columns), F32),
        ],
        compiler_params=pltpu.CompilerParams(vmem_limit_bytes=VMEM_LIMIT),
        cost_estimate=cost(flops, 4 * 1024 * 1024),
        name="backward",
    )(rest, others, from_chip, waves, own_rows, weights)


def iterate(plain, target, one, two, primal, part, span, last_rows):
    blocks = plain.shape[1]
    scale = DUAL_STEP / TV_WEIGHT
    lane = lax.broadcasted_iota(jnp.int32, (GROUP, LANES), 1)
    row = lax.broadcasted_iota(jnp.int32, (GROUP, LANES), 0)
    left_edge, right_edge = lane == 0, lane == LANES - 1
    zero = jnp.zeros((GROUP, LANES), F32)

    def at(ref, step):
        return [ref[part, b, step] for b in range(blocks)]

    def primal_of(duals, step, previous):
        dual, cols, base = at(duals[0], step), at(duals[1], step), at(target, step)
        turned = [pltpu.roll(v, 1, 1) for v in cols]
        result = []
        for b in range(blocks):
            moved = jnp.where(left_edge, turned[b - 1] if b else zero, turned[b])
            diverged = (dual[b] - previous[b]) + (cols[b] - moved)
            result.append(base[b] + (scale * TV_WEIGHT) * diverged)
        return result, dual

    def before_first(duals):
        return [jnp.where(row == 0, 0.0, pltpu.roll(v, 1, 0)) for v in at(duals[0], span - 1)]

    def ascend(duals, results, value, after, step):
        turned = [pltpu.roll(v, LANES - 1, 1) for v in value]
        dual, cols = (at(ref, step) for ref in duals) if duals else (None, None)
        for b in range(blocks):
            below = after[b]
            if step in last_rows:
                below = jnp.where(last_rows[step], value[b], below)
            right = turned[b + 1] if b + 1 < blocks else value[b]
            right = jnp.where(right_edge, right, turned[b])
            new_rows, new_cols = below - value[b], right - value[b]
            if duals:
                new_rows, new_cols = dual[b] + new_rows, cols[b] + new_cols
            shrink = jnp.minimum(1.0, lax.rsqrt(new_rows * new_rows + new_cols * new_cols))
            results[0][part, b, step] = new_rows * shrink
            results[1][part, b, step] = new_cols * shrink

    def sweep(duals, results):
        previous = before_first(duals)
        for step in range(span):
            value, previous = primal_of(duals, step, previous)
            for b in range(blocks):
                primal[part, b, step] = value[b]
                if step == 0:
                    primal[part, b, span] = pltpu.roll(value[b], GROUP - 1, 0)
        for step in range(span):
            ascend(duals, results, at(primal, step), at(primal, step + 1), step)

    values = [[plain[part, b, pl.ds(step, GROUP, stride=span), :] for b in range(blocks)] for step in range(2)]
    wrapped = [pltpu.roll(v, GROUP - 1, 0) for v in values[0]]
    for step in range(span):
        value, after = values
        for b in range(blocks):
            target[part, b, step] = value[b]
        ascend(None, one, value, after, step)
        if step + 2 < span:
            following = [plain[part, b, pl.ds(step + 2, GROUP, stride=span), :] for b in range(blocks)]
        else:
            following = wrapped
        values = [after, following]

    def twice(_, carry):
        sweep(one, two)
        sweep(two, one)
        return carry

    for _ in range((TV_ITERS - 1) // 2):
        twice(0, 0)
    last = one
    if TV_ITERS % 2 == 0:
        sweep(one, two)
        last = two
    previous = before_first(last)
    for step in range(span):
        result, previous = primal_of(last, step, previous)
        for b in range(blocks):
            plain[part, b, pl.ds(step, GROUP, stride=span), :] = result[b]


def denoise_scratch(span, blocks):
    buffer = pltpu.VMEM((2, blocks, span, GROUP, LANES), F32)
    return [
        pltpu.VMEM((2, blocks, span * GROUP, LANES), F32),
        buffer,
        buffer,
        buffer,
        buffer,
        buffer,
        pltpu.VMEM((2, blocks, span + 1, GROUP, LANES), F32),
    ]


def denoise(target_rows, from_chip):
    groups, _, columns = target_rows.shape
    groups = groups // 2
    rows = groups * GROUP
    span, blocks = groups + 2, columns // LANES
    tiles = lax.axis_size("tile")
    scale = DUAL_STEP / TV_WEIGHT
    above_at = divmod(GROUP - 1, span)
    last_at = divmod(GROUP + rows - 1, span)

    def kernel(
        pieces, chip, out, plain, target, rows_one, cols_one, rows_two, cols_two, primal, result, sems
    ):
        tile = lax.axis_index("tile")
        is_odd = tile % 2 == 1
        row = lax.broadcasted_iota(jnp.int32, (GROUP, LANES), 0)
        last_rows = {
            above_at[1]: (row == above_at[0]) & (tile == 0),
            last_at[1]: (row == last_at[0]) & (tile == tiles - 1),
        }
        start = 1 - tile % 2
        values = [jnp.where(is_odd, chip[1], pieces[2 * groups - 2])]
        values += [pieces[2 * group + start] for group in range(groups)]
        values += [jnp.where(is_odd, pieces[1], chip[0])]
        for group, value in enumerate(values):
            value = scale * value.astype(F32)
            at = slice(group * GROUP, (group + 1) * GROUP)
            for b in range(blocks):
                lanes = slice(b * LANES, (b + 1) * LANES)
                plain[0, b, at] = value[:GROUP, lanes]
                plain[1, b, at] = value[GROUP:, lanes]
        copies = []
        for part in range(2):
            iterate(
                plain, target, (rows_one, cols_one), (rows_two, cols_two), primal, part, span, last_rows
            )
            for b in range(blocks):
                result[part, :, b * LANES : (b + 1) * LANES] = plain[part, b, GROUP : GROUP + rows] * (
                    1.0 / scale
                )
            copies.append(pltpu.make_async_copy(result.at[part], out.at[part, 0], sems.at[part]))
            copies[-1].start()
        for copy in copies:
            copy.wait()

    return pl.pallas_call(
        kernel,
        out_shape=jax.ShapeDtypeStruct((2, 1, rows, columns), F32),
        in_specs=[whole()] * 2,
        out_specs=whole(pltpu.HBM),
        scratch_shapes=denoise_scratch(span, blocks)
        + [pltpu.VMEM((2, rows, columns), F32), pltpu.SemaphoreType.DMA((2,))],
        compiler_params=pltpu.CompilerParams(vmem_limit_bytes=VMEM_LIMIT),
        cost_estimate=cost(0, 4 * 1024 * 1024),
        name="denoise",
    )(target_rows, from_chip)


def exchanged(value, tiles, scans):
    groups = [
        [tile % tiles * scans + scan for scan in range(scans) for tile in (odd, odd + 1)]
        for odd in range(1, tiles, 2)
    ]
    return lax.all_to_all(value, ("tile", "scan"), 0, 0, tiled=True, axis_index_groups=groups)


def per_device(object_slices, probe_wave, propagator, offsets, adjoint):
    classes = probe_wave.shape[1] // STRIDE
    tiles, scans = lax.axis_size("tile"), lax.axis_size("scan")
    send = spread(offsets, adjoint)
    received = exchanged(send, tiles, scans)
    own_rows = pick(object_slices, send)
    waves = forward(own_rows, probe_wave, propagator, classes)
    late = range(1, classes)
    others = sum_by_offset(received, waves, classes, [(0, step) for step in late], "others")
    from_chip = swapped(others)
    rest = sum_by_offset(received, others, classes, [(0, 0)] + [(1, step) for step in late], "rest")
    weights = adjoint_weights(propagator, others)
    chunks = backward(rest, others, from_chip, waves, own_rows, weights, classes)
    target_rows = exchanged(chunks, tiles, scans)
    outward = jnp.concatenate([target_rows[:1], target_rows[-1:]], axis=0)
    return denoise(target_rows, swapped(outward))


def solution(mesh):
    in_specs = (
        P(None, None, "tile", None),
        P(),
        P(),
        P("tile", "scan"),
        P(None, "tile", "scan", None, None),
    )
    out_specs = P(None, "scan", "tile", None)
    return jax.shard_map(
        per_device, mesh=mesh, in_specs=in_specs, out_specs=out_specs, check_vma=False
    )
```
